32 devices in a mesh: tile: 16 (over z, x, core), lev: 2 (over y).
Axes of the slice: x: 2, y: 2, z: 4, core: 2. Of those that a mesh axis runs over, the one named last changes fastest.
Arguments:
- gradient: float32 [144, 2, 256, 640], P('lev', None, 'tile'), may hold values from -6 to 6
- land_sea: int32 [144, 256, 640], P('lev', 'tile'), may hold values 0 or 1
- roughness: float32 [144, 256, 640], P('lev', 'tile'), may hold values from 0.5 to 1.4
- scale_index: int32 [10, 144], replicated, may hold values from 0 to 7
- scale_table: float32 [8], replicated, may hold values from 0.03 to 0.12
- balance: float32 [144, 144], replicated, may hold values from -0.5 to 0.5
- corr_a: float32 [144, 144], replicated, may hold values from -0.5 to 0.5
- corr_b: float32 [144, 144], replicated, may hold values from -0.5 to 0.5
Outputs:
- control_grad: float32 [144, 2, 256, 640], P('lev', None, 'tile')
The draws below stay inside these ranges and needn't reach their ends.
All inputs are finite; a program needn't handle non-finite values. No bound on the sum of `land_sea` on one device may be relied on, other than what follows from the above.
Results may differ from the reference program's by a relative error of at most 0.000098.
Values sent between devices are 32-bit elements; how exact they have to be, the bound alone decides.
No kernel may reach another device: no remote copies, remote signals or barrier semaphores. Data moves between devices by JAX's collectives and lax.ppermute only.
A program may use at most 128 MiB of HBM per device.

```python
import jax
import jax.numpy as jnp
from jax import lax

LEV = 144
LAT = 640
PASSES = 10
NSCALE = 8
LON = 256


def draw_roughness(key, part):
    key = jax.random.fold_in(key, 11)
    unit = jax.random.uniform(key, (LEV, LON, LAT), jnp.float32)
    return 0.5 * jnp.exp(unit * jnp.log(2.8))


def draw_scale_table(key, part):
    key = jax.random.fold_in(key, 23)
    unit = jax.random.uniform(key, (NSCALE,), jnp.float32)
    return 0.03 * jnp.exp(unit * jnp.log(4.0))


def set_ends(array, rng, low, high):
    extent = array.shape
    place = [jax.random.randint(jax.random.fold_in(rng, axis), (), 0, extent[axis]) for axis in range(len(extent))]
    array = array.at[tuple(place)].set(low)
    longest = extent.index(max(extent))
    place[longest] = (place[longest] + 1) % extent[longest]
    return array.at[tuple(place)].set(high)


def block_levels(stream_key, shape, pieces, least, top_value):
    def one(axis_at, parts):
        heights = jax.random.uniform(jax.random.fold_in(jax.random.fold_in(stream_key, 6), axis_at), (parts,), jnp.float32, least / len(pieces), top_value / len(pieces))
        return jnp.repeat(jnp.exp(heights), shape[axis_at] // parts).reshape((-1,) + (1,) * (len(shape) - axis_at - 1))

    factor_of = one(*pieces[0])
    for cut in pieces[1:]:
        factor_of = factor_of * one(*cut)
    return factor_of


def normal_values(own_key, extent, deviation, bound, cuts=(), held_as=jnp.bfloat16):
    values = jax.random.normal(own_key, extent, jnp.float32) * deviation
    if len(cuts) > 0:
        values = block_levels(own_key, extent, cuts, -0.22, 0.18) * values
    return jnp.clip(values, min=-bound, max=bound).astype(held_as)


def setup_inputs(seed: int = 0) -> dict:
    streams_of = jax.random.split(jax.random.key(seed), 9)
    gradient = normal_values(streams_of[0], (LEV, 2, LON, LAT), 1.0, 6.0, ((0, 2), (2, 16)), jnp.float32)
    land_sea = set_ends((jax.random.randint(streams_of[1], (LEV, LON, LAT), 0, 16) < 15).astype(jnp.int32), jax.random.fold_in(streams_of[1], 1), 0, 1)
    roughness = draw_roughness(jax.random.fold_in(streams_of[8], 71), 0)
    scale_index = set_ends(jax.random.randint(streams_of[3], (PASSES, LEV), 0, NSCALE), jax.random.fold_in(streams_of[3], 1), 0, NSCALE - 1).astype(jnp.int32)
    scale_table = draw_scale_table(jax.random.fold_in(streams_of[8], 71), 0)
    balance = normal_values(streams_of[5], (LEV, LEV), LEV ** -0.5, 0.5, (), jnp.float32)
    corr_a = normal_values(streams_of[6], (LEV, LEV), LEV ** -0.5, 0.5, (), jnp.float32)
    corr_b = normal_values(streams_of[7], (LEV, LEV), LEV ** -0.5, 0.5, (), jnp.float32)
    return dict(gradient=gradient, land_sea=land_sea, roughness=roughness, scale_index=scale_index, scale_table=scale_table, balance=balance, corr_a=corr_a, corr_b=corr_b)


def lat_spread(weighted):
    upper = jnp.concatenate([weighted[..., 1:], weighted[..., -1:]], -1)
    lower = jnp.concatenate([weighted[..., :1], weighted[..., :-1]], -1)
    return upper + lower - 2.0 * weighted


def reference(gradient, land_sea, roughness, scale_index, scale_table, balance, corr_a, corr_b):
    exact = lax.Precision.HIGHEST
    first_var = gradient[:, 0]
    second_var = gradient[:, 1]
    first = first_var + jnp.einsum("ml,mxy->lxy", balance, second_var, precision=exact)
    out_a = jnp.einsum("lk,lxy->kxy", corr_a, first, precision=exact)
    out_b = jnp.einsum("lk,lxy->kxy", corr_b, second_var, precision=exact)
    field = jnp.stack([out_a, out_b], 1)
    coef = (land_sea.astype(jnp.float32) * roughness)[:, None]
    picks = (scale_index[:, :, None] == jnp.arange(NSCALE, dtype=jnp.int32)[None, None, :]).astype(jnp.float32)
    rates = jnp.sum(picks * scale_table[None, None, :], -1)
    for section in range(PASSES):
        weighted = coef * field
        spread = jnp.roll(weighted, 1, 2) + jnp.roll(weighted, -1, 2) - 2.0 * weighted + lat_spread(weighted)
        field = field + rates[section][:, None, None, None] * coef * spread
    return field
```

```python
import functools

import jax
import jax.numpy as jnp
import numpy as np
from jax import lax
from jax.experimental import pallas as pl
from jax.experimental.pallas import tpu as pltpu
from jax.sharding import PartitionSpec as P

PASSES = 10
NSCALE = 8
ROWS = 8
LANES = 128
PAIR = 2
EXACT = lax.Precision.HIGHEST
VMEM_LIMIT = 50 * 1024 * 1024


def chunk_units(total):
    return [2] * (total // 2) + [1] * (total % 2)


def lane_tile(j):
    return slice(j * LANES, (j + 1) * LANES)


def dot_t(a, b):
    return lax.dot_general(
        a, b, (((1,), (1,)), ((), ())), precision=EXACT, preferred_element_type=jnp.float32
    )


def halve(value):
    high = value.astype(jnp.bfloat16)
    return high, (value - high.astype(jnp.float32)).astype(jnp.bfloat16)


def pick_levels(rows, levels, padded, own, starts):
    row = lax.broadcasted_iota(jnp.int32, (rows, levels), 0)
    col = lax.broadcasted_iota(jnp.int32, (rows, levels), 1)
    picked = jnp.zeros((rows, levels), jnp.bool_)
    for s, start in enumerate(starts):
        if start is not None:
            at = row - s * padded
            picked = picked | ((at >= 0) & (at < own) & (col == at + start))
    return picked.astype(jnp.float32)


def three_parts(full, third):
    high, low = halve(full)
    part = lax.broadcasted_iota(jnp.int32, full.shape, 1)
    return jnp.where(part < 2 * third, high.astype(jnp.float32), low.astype(jnp.float32)).astype(jnp.bfloat16)


def dot_exact(a, b):
    return jnp.dot(a, b, precision=EXACT, preferred_element_type=jnp.float32)


def dot_half(a, b):
    return jnp.dot(a, b, preferred_element_type=jnp.float32)


def ordered_parts(lines, plain, order, halves):
    rows, lats = lines.shape[1:]
    for side in range(PAIR):
        high, low = halve(lines[side])
        plain[2 * side * rows : (2 * side + 1) * rows, :] = high
        plain[(2 * side + 1) * rows : (2 * side + 2) * rows, :] = low
    ordered = dot_half(plain[...], order[...])
    for side in range(PAIR):
        place = slice(side * lats, (side + 1) * lats)
        both = ordered[2 * side * rows : 2 * (side + 1) * rows].astype(jnp.bfloat16)
        halves[0 : 2 * rows, place] = both
        halves[2 * rows : 3 * rows, place] = both[0:rows]


def plane(lons, lon, var):
    side, at = divmod(lon, lons // 2)
    group, place = divmod(at, PAIR)
    if side == 0:
        return 3 * PAIR * group + place if var == 0 else None
    return 3 * PAIR * group + PAIR + 2 * place + var


def mix_kernel(shape, offsets, at, *refs):
    levels, own, padded, lons, tiles, targets = shape
    grads, (bal, cor_a, cor_b, order, _), refs = refs[:tiles], refs[tiles : tiles + 5], refs[tiles + 5 :]
    outs, (weight, weight_raw, lines, plain, halves) = refs[:-5], refs[-5:]
    lats = tiles * LANES
    step = pl.program_id(0)

    @pl.when(step == 0)
    def _():
        first = [at[0], None] * 3
        second = [None, at[0]] * 3
        take_first = pick_levels(6 * padded, levels, padded, own, first)
        take_second = pick_levels(6 * padded, levels, padded, own, second)
        pick = pick_levels(targets * padded, levels, padded, own, [at[t] for t in range(targets)])
        cols_a = dot_t(pick, cor_a[...])
        through_a = dot_t(cols_a, take_first + dot_exact(take_second, bal[...]))
        through_b = dot_t(dot_t(pick, cor_b[...]), take_second)
        only_first = dot_t(cols_a, take_first)
        weight[...] = three_parts(jnp.concatenate([through_a, through_b], 0), 2 * padded)
        weight_raw[...] = three_parts(
            jnp.concatenate([through_a[:padded], only_first[padded:], through_b[:padded]], 0), 2 * padded
        )
        lines[...] = jnp.zeros_like(lines)

    for half in range(2):
        for side in range(PAIR):
            lon = half * (lons // 2) + step * PAIR + side
            for var in range(2):
                for j, grad in enumerate(grads):
                    lines[half, side, pl.ds(var * padded, own), lane_tile(j)] = grad[
                        pl.ds(var * lons + lon, own, stride=2 * lons), :
                    ]
        ordered_parts(lines.at[half], plain.at[half], order, halves.at[half])
    for half in range(2):
        mixed = dot_half((weight_raw if half == 0 else weight)[...], halves[half])
        for side in range(PAIR):
            place = slice(side * lats, (side + 1) * lats)
            for target in range(targets):
                for var in range(2):
                    if half == 0 and target > 0 and var == 1:
                        continue
                    first = (var * targets + target) * padded
                    for c, (start, size) in enumerate(offsets):
                        out = outs[target * len(offsets) + c]
                        value = mixed[first + start : first + start + size, place]
                        if target == 0:
                            out[half, side, var] = value
                        else:
                            out[plane(lons, half * (lons // 2) + side, var)] = value


def raw_kernel(shape, offsets, at, *refs):
    levels, own, padded, lons, tiles, targets = shape
    chunks = len(offsets)
    raws, refs = refs[: tiles * (targets - 1)], refs[tiles * (targets - 1) :]
    (bal, cor_a, cor_b, order), kept, outs = refs[:4], refs[4 : 4 + chunks], refs[4 + chunks : 4 + 2 * chunks]
    weight, lines, plain, halves = refs[4 + 2 * chunks :]
    lats = tiles * LANES
    step = pl.program_id(0)

    @pl.when(step == 0)
    def _():
        pick = pick_levels(padded, levels, padded, own, [at[0]])
        cols_a = dot_t(pick, cor_a[...])
        cols_b = dot_t(pick, cor_b[...])
        for source in range(1, targets):
            take = pick_levels(3 * padded, levels, padded, own, [at[source]] * 3)
            full = jnp.concatenate([dot_t(cols_a, dot_exact(take, bal[...])), dot_t(cols_b, take)], 0)
            weight[source - 1] = three_parts(full, padded)
        lines[...] = jnp.zeros_like(lines)

    total = None
    for source in range(targets - 1):
        for side in range(PAIR):
            for j in range(tiles):
                lines[side, 0:own, lane_tile(j)] = raws[source * tiles + j][
                    pl.ds(step * PAIR + side, own, stride=lons // 2), :
                ]
        ordered_parts(lines, plain, order, halves)
        mixed = dot_half(weight[source], halves[...])
        total = mixed if total is None else total + mixed
    for side in range(PAIR):
        place = slice(side * lats, (side + 1) * lats)
        for var in range(2):
            for (start, size), more, out in zip(offsets, kept, outs):
                first = var * padded + start
                out[0, side, var] = more[0, side, var] + total[first : first + size, place]


def coef_kernel(own, padded, lons, halo, tiles, *refs):
    seas, roughs, (order, _, coef, first, last, lines) = refs[:tiles], refs[tiles : 2 * tiles], refs[2 * tiles :]
    half = lons // 2
    lines[...] = jnp.zeros_like(lines)
    for group in range(2):
        for at in range(half):
            rows = pl.ds(group * half + at, own, stride=lons)
            for j in range(tiles):
                lines[at * padded : at * padded + own, lane_tile(j)] = (
                    seas[j][rows, :].astype(jnp.float32) * roughs[j][rows, :]
                )
        high, low = halve(lines[...])
        value = jnp.dot(high, order[...], preferred_element_type=jnp.float32) + jnp.dot(
            low, order[...], preferred_element_type=jnp.float32
        )
        for at in range(half):
            lon = group * half + at
            piece = value[at * padded : (at + 1) * padded]
            coef[lon] = piece
            if lon < halo:
                first[lon] = piece
            if lon >= lons - halo:
                last[lon - (lons - halo)] = piece


def mixed_at(lons, sums, lon, var):
    value = sums[0][lon // (lons // 2), lon % (lons // 2), var]
    at = plane(lons, lon, var)
    if at is not None:
        for more in sums[1:]:
            value = value + more[at]
    return value


def edge_kernel(lons, halo, parts, passed, *refs):
    sums, coef, (first, last, token) = refs[:parts], refs[parts], refs[parts + 4 + passed : parts + 7 + passed]
    token[...] = jnp.zeros_like(token)
    for lon in range(lons):
        for var in range(2):
            value = coef[lon] * mixed_at(lons, sums, lon, var)
            if lon < halo:
                first[lon, var] = value
            if lon >= lons - halo:
                last[lon - (lons - halo), var] = value


def neighbours(tiles, lane):
    count = len(tiles)
    before = jnp.where(lane == 0, tiles[0], pltpu.roll(tiles[-1], 1, 1))
    after = jnp.where(lane == LANES - 1, tiles[-1], pltpu.roll(tiles[0], LANES - 1, 1))
    line = [before, *tiles, after]
    return [line[j] + line[j + 2] for j in range(count)]


def diffuse(lons, lats, sums, coef, before, after, coef_before, coef_after, rates, weighted, square):
    halo = PASSES
    tiles = lats // LANES
    lane = lax.broadcasted_iota(jnp.int32, (ROWS, LANES), 1)

    for lon in range(lons):
        scale = coef[lon]
        square[halo + lon] = scale * scale
        for var in range(2):
            weighted[0][halo + lon, var] = scale * mixed_at(lons, sums, lon, var)
    for lon in range(halo):
        weighted[0][lon] = before[lon]
        weighted[0][halo + lons + lon] = after[lon]
    for lon in range(halo - 1):
        square[1 + lon] = coef_before[lon] * coef_before[lon]
        square[halo + lons + lon] = coef_after[lon] * coef_after[lon]

    for section in range(PASSES):
        source, target = weighted[section % 2], weighted[(section + 1) % 2]
        rate = rates[section]
        count = (lons + 2 * halo - 2 * section - 2) // 2

        def load(lon):
            return [[source[lon, var, :, lane_tile(j)] for j in range(tiles)] for var in range(2)]

        def part(at, carry):
            start = section + 1 + at * count
            behind, here = load(start - 1), load(start)
            for lon in range(count):
                ahead = load(start + lon + 1)
                factor = [rate * square[start + lon, :, lane_tile(j)] for j in range(tiles)]
                for var in range(2):
                    lat = neighbours(here[var], lane)
                    for j in range(tiles):
                        spread = (behind[var][j] + ahead[var][j]) + lat[j] - 4.0 * here[var][j]
                        target[start + lon, var, :, lane_tile(j)] = here[var][j] + factor[j] * spread
                behind, here = here, ahead
            return carry

        lax.fori_loop(0, 2, part, 0)


def diffuse_kernel(lons, lats, parts, *refs):
    sums, rest = refs[:parts], refs[parts:]
    coef, before, after, coef_before, coef_after, rates, back, _, _, out, token, *rest = rest
    *weighted, square, lines = rest
    tiles = lats // LANES
    token[...] = jnp.zeros_like(token)
    diffuse(lons, lats, sums, coef, before, after, coef_before, coef_after, rates, weighted, square)

    count = ROWS * 2 * lons
    for lon in range(lons):
        scale = coef[lon]
        land = scale == 0.0
        inverse = 1.0 / jnp.where(land, 1.0, scale)
        for var in range(2):
            plain = mixed_at(lons, sums, lon, var)
            value = jnp.where(land, plain, weighted[PASSES % 2][PASSES + lon, var] * inverse)
            for j in range(tiles):
                lines[pl.ds(j * count + var * lons + lon, ROWS, stride=2 * lons), :] = value[:, lane_tile(j)]
    high, low = halve(jnp.concatenate([lines[j * count : (j + 1) * count, :] for j in range(tiles)], 1))
    out[...] = jnp.dot(high, back[...], preferred_element_type=jnp.float32) + jnp.dot(
        low, back[...], preferred_element_type=jnp.float32
    )


def whole(*block):
    return pl.BlockSpec(block, lambda i: (0,) * len(block))


def params():
    return pltpu.CompilerParams(vmem_limit_bytes=VMEM_LIMIT)


def spent(microseconds):
    return pl.CostEstimate(flops=int(microseconds * 1.153e9), bytes_accessed=1024, transcendentals=0)


def on_device(gradient, land_sea, roughness, scale_index, scale_table, balance, corr_a, corr_b):
    own, _, lons, lats = gradient.shape
    levels = balance.shape[0]
    lev_count = lax.axis_size("lev")
    tile_count = lax.axis_size("tile")
    me = lax.axis_index("lev")
    units = -(-own // ROWS)
    padded = units * ROWS
    chunks = chunk_units(units)
    starts = [sum(chunks[:c]) for c in range(len(chunks))]
    offsets = [(s * ROWS, c * ROWS) for s, c in zip(starts, chunks)]
    halo = PASSES
    unit_bytes = lons * 2 * ROWS * lats * 4
    f32 = jnp.float32

    def along(shift):
        return [(i, (i + shift) % lev_count) for i in range(lev_count)]

    with jax.named_scope("raw"):
        rows = gradient[:, 1, : lons // 2]
        raws = [lax.ppermute(rows, "lev", along(shift)) for shift in range(1, lev_count)]

    tiles = lats // LANES
    place = np.arange(lats)
    order = np.zeros((lats, lats), np.float32)
    order[place, (place % tiles) * LANES + place // tiles] = 1.0
    back = jnp.asarray(order.T, jnp.bfloat16)
    order = jnp.asarray(order, jnp.bfloat16)

    up = [(i, (i + 1) % tile_count) for i in range(tile_count)]
    down = [(j, i) for i, j in up]
    with jax.named_scope("coef"):
        coef, first, last = pl.pallas_call(
            functools.partial(coef_kernel, own, padded, lons, halo - 1, tiles),
            grid=(1,),
            out_shape=[
                jax.ShapeDtypeStruct((lons, padded, lats), f32),
                jax.ShapeDtypeStruct((halo - 1, padded, lats), f32),
                jax.ShapeDtypeStruct((halo - 1, padded, lats), f32),
            ],
            in_specs=[pl.BlockSpec((own * lons, LANES), lambda i, j=j: (0, j)) for j in range(tiles)] * 2
            + [whole(lats, lats), pl.BlockSpec(memory_space=pl.ANY)],
            out_specs=[
                whole(lons, padded, lats),
                whole(halo - 1, padded, lats),
                whole(halo - 1, padded, lats),
            ],
            scratch_shapes=[pltpu.VMEM((lons // 2 * padded, lats), f32)],
            compiler_params=params(),
            cost_estimate=spent(10),
            name="coef",
        )(
            *[land_sea.reshape(own * lons, lats)] * tiles,
            *[roughness.reshape(own * lons, lats)] * tiles,
            order,
            rows,
        )
        coef_before = lax.ppermute(last, "tile", up)
        coef_after = lax.ppermute(first, "tile", down)

    half = lons // 2
    shape = (levels, own, padded, lons, tiles, lev_count)
    kept_shapes = [jax.ShapeDtypeStruct((2, half, 2, size, lats), f32) for _, size in offsets]
    sent_shapes = [jax.ShapeDtypeStruct((3 * half, size, lats), f32) for _, size in offsets]
    kept_specs = [pl.BlockSpec((2, PAIR, 2, size, lats), lambda i: (0, i, 0, 0, 0)) for _, size in offsets]
    sent_specs = [pl.BlockSpec((3 * PAIR, size, lats), lambda i: (i, 0, 0)) for _, size in offsets]
    level_starts = [lax.rem(me + shift, lev_count) * own for shift in range(lev_count)]
    with jax.named_scope("mix"):
        mixed = pl.pallas_call(
            functools.partial(mix_kernel, shape, offsets),
            grid=(half // PAIR,),
            out_shape=kept_shapes + sent_shapes * (lev_count - 1),
            in_specs=[pl.BlockSpec(memory_space=pltpu.SMEM)]
            + [pl.BlockSpec((own * 2 * lons, LANES), lambda i, j=j: (0, j)) for j in range(tiles)]
            + [whole(levels, levels)] * 3
            + [whole(lats, lats), pl.BlockSpec(memory_space=pl.ANY)],
            out_specs=kept_specs + sent_specs * (lev_count - 1),
            scratch_shapes=[
                pltpu.VMEM((2 * lev_count * padded, 6 * padded), jnp.bfloat16),
                pltpu.VMEM(((lev_count + 1) * padded, 6 * padded), jnp.bfloat16),
                pltpu.VMEM((2, PAIR, 2 * padded, lats), f32),
                pltpu.VMEM((2, PAIR * 4 * padded, lats), jnp.bfloat16),
                pltpu.VMEM((2, 6 * padded, PAIR * lats), jnp.bfloat16),
            ],
            compiler_params=params(),
            cost_estimate=spent(20),
            name="mix",
        )(
            jnp.stack(level_starts),
            *[gradient.reshape(own * 2 * lons, lats)] * tiles,
            balance,
            corr_a,
            corr_b,
            order,
            first,
        )
        sent = [mixed[c + len(chunks) :: len(chunks)] for c in range(len(chunks))]

        def send(arrays):
            return [lax.ppermute(array, "lev", along(shift + 1)) for shift, array in enumerate(arrays)]

        final = len(chunks) - 1
        received = [send(arrays) if c < final or final < 2 else None for c, arrays in enumerate(sent)]
        kept = pl.pallas_call(
            functools.partial(raw_kernel, shape, offsets),
            grid=(half // PAIR,),
            out_shape=kept_shapes,
            in_specs=[pl.BlockSpec(memory_space=pltpu.SMEM)]
            + [pl.BlockSpec((own * half, LANES), lambda i, j=j: (0, j)) for j in range(tiles)] * (lev_count - 1)
            + [whole(levels, levels)] * 3
            + [whole(lats, lats)]
            + [pl.BlockSpec((1, PAIR, 2, size, lats), lambda i: (0, i, 0, 0, 0)) for _, size in offsets],
            out_specs=[pl.BlockSpec((1, PAIR, 2, size, lats), lambda i: (0, i, 0, 0, 0)) for _, size in offsets],
            scratch_shapes=[
                pltpu.VMEM((lev_count - 1, 2 * padded, 3 * padded), jnp.bfloat16),
                pltpu.VMEM((PAIR, padded, lats), f32),
                pltpu.VMEM((PAIR * 2 * padded, lats), jnp.bfloat16),
                pltpu.VMEM((3 * padded, PAIR * lats), jnp.bfloat16),
            ],
            input_output_aliases={5 + tiles * (lev_count - 1) + c: c for c in range(len(chunks))},
            compiler_params=params(),
            cost_estimate=spent(6),
            name="raw",
        )(
            jnp.stack([level_starts[(lev_count - shift) % lev_count] for shift in range(lev_count)]),
            *[part for raw in raws for part in [raw.reshape(own * half, lats)] * tiles],
            balance,
            corr_a,
            corr_b,
            order,
            *mixed[: len(chunks)],
        )

    with jax.named_scope("rates"):
        own_index = lax.dynamic_slice_in_dim(scale_index, me * own, own, 1)
        picks = own_index[:, :, None] == jnp.arange(NSCALE, dtype=jnp.int32)[None, None, :]
        rates = jnp.sum(picks.astype(f32) * scale_table[None, None, :], -1)
        rates = jnp.pad(rates, ((0, 0), (0, padded - own)))
        rates = jnp.broadcast_to(rates[:, :, None], (PASSES, padded, LANES))

    token_shape = jax.ShapeDtypeStruct((ROWS, LANES), f32)
    token_spec = pl.BlockSpec((ROWS, LANES), lambda i: (0, 0))
    hidden = pl.BlockSpec(memory_space=pl.ANY)
    result = jnp.zeros((ROWS, LANES), f32)
    token = result

    def sum_specs(parts):
        own_sum = pl.BlockSpec((2, half, 2, ROWS, lats), lambda i: (0, 0, 0, i, 0))
        return [own_sum] + [pl.BlockSpec((3 * half, ROWS, lats), lambda i: (0, i, 0))] * (parts - 1)

    def edges(c, token, passed):
        sums = [kept[c]] + received[c]
        count, start = chunks[c], starts[c]
        halo_shape = jax.ShapeDtypeStruct((halo, 2, count * ROWS, lats), f32)
        fixed = [jax.ShapeDtypeStruct(array.shape, array.dtype) for array in passed]
        with jax.named_scope("edges"):
            first, last, token, *passed = pl.pallas_call(
                functools.partial(edge_kernel, lons, halo, len(sums), len(passed)),
                grid=(count,),
                out_shape=[halo_shape, halo_shape, token_shape, *fixed],
                in_specs=sum_specs(len(sums))
                + [pl.BlockSpec((lons, ROWS, lats), lambda i: (0, start + i, 0))]
                + [hidden] * (3 + len(passed)),
                out_specs=[pl.BlockSpec((halo, 2, ROWS, lats), lambda i: (0, 0, i, 0))] * 2
                + [token_spec]
                + [hidden] * len(passed),
                input_output_aliases={len(sums) + 4 + i: 3 + i for i in range(len(passed))},
                compiler_params=params(),
                cost_estimate=spent(2),
                name="edges",
            )(*sums, coef, coef_before, coef_after, token, *passed)
            return lax.ppermute(last, "tile", up), lax.ppermute(first, "tile", down), token, passed

    def diffusion(c, before, after, result, token):
        sums = [kept[c]] + received[c]
        count, start = chunks[c], starts[c]
        fixed = lambda i: (0, 0, i, 0)
        level = lambda i: (0, start + i, 0)
        operands = [*sums, coef, before, after, coef_before, coef_after, rates, back, token, result]
        with jax.named_scope("diffusion"):
            return pl.pallas_call(
                functools.partial(diffuse_kernel, lons, lats, len(sums)),
                grid=(count,),
                out_shape=[jax.ShapeDtypeStruct((own * 2 * lons, lats), f32), token_shape],
                in_specs=sum_specs(len(sums))
                + [pl.BlockSpec((lons, ROWS, lats), level)]
                + [pl.BlockSpec((halo, 2, ROWS, lats), fixed)] * 2
                + [pl.BlockSpec((halo - 1, ROWS, lats), level)] * 2
                + [pl.BlockSpec((PASSES, ROWS, LANES), level), whole(lats, lats), hidden, hidden],
                out_specs=[pl.BlockSpec((ROWS * 2 * lons, lats), lambda i: (start + i, 0)), token_spec],
                scratch_shapes=[
                    pltpu.VMEM((lons + 2 * halo, 2, ROWS, lats), f32),
                    pltpu.VMEM((lons + 2 * halo, 2, ROWS, lats), f32),
                    pltpu.VMEM((lons + 2 * halo, ROWS, lats), f32),
                    pltpu.VMEM((tiles * ROWS * 2 * lons, LANES), f32),
                ],
                input_output_aliases={} if c == 0 else {len(operands) - 1: 0},
                compiler_params=params(),
                cost_estimate=spent(11),
                name="diffusion",
            )(*operands)

    waiting = None
    for c in range(len(chunks)):
        before, after, token, passed = edges(c, token, sent[final] if c == final - 2 else [])
        if c == final - 2:
            received[final] = send(passed)
        if waiting is not None:
            result, token = diffusion(c - 1, *waiting, result, token)
        waiting = (before, after)
    result, _ = diffusion(len(chunks) - 1, *waiting, result, token)
    return result.reshape(own, 2, lons, lats)


def solution(mesh):
    return jax.shard_map(
        on_device,
        mesh=mesh,
        in_specs=(
            P("lev", None, "tile", None),
            P("lev", "tile", None),
            P("lev", "tile", None),
            P(),
            P(),
            P(),
            P(),
            P(),
        ),
        out_specs=P("lev", None, "tile", None),
        check_vma=False,
    )
```

```python
import functools

import jax
import jax.numpy as jnp
import numpy as np
from jax import lax
from jax.experimental import pallas as pl
from jax.experimental.pallas import tpu as pltpu
from jax.sharding import PartitionSpec as P

PASSES = 10
NSCALE = 8
ROWS = 8
LANES = 128
COEF_GROUPS = 4
PAIR = 2
EXACT = lax.Precision.HIGHEST
VMEM_LIMIT = 65200 * 1024


def chunk_units(total):
    return [2] * (total // 2) + [1] * (total % 2)


def lane_tile(j):
    return slice(j * LANES, (j + 1) * LANES)


def dot_t(a, b):
    return lax.dot_general(
        a, b, (((1,), (1,)), ((), ())), precision=EXACT, preferred_element_type=jnp.float32
    )


def halve(value):
    high = value.astype(jnp.bfloat16)
    return high, (value - high.astype(jnp.float32)).astype(jnp.bfloat16)


def pick_levels(rows, levels, padded, own, starts):
    row = lax.broadcasted_iota(jnp.int32, (rows, levels), 0)
    col = lax.broadcasted_iota(jnp.int32, (rows, levels), 1)
    picked = jnp.zeros((rows, levels), jnp.bool_)
    for s, start in enumerate(starts):
        if start is not None:
            at = row - s * padded
            picked = picked | ((at >= 0) & (at < own) & (col == at + start))
    return picked.astype(jnp.float32)


def three_parts(full, third):
    high, low = halve(full)
    part = lax.broadcasted_iota(jnp.int32, full.shape, 1)
    return jnp.where(part < 2 * third, high.astype(jnp.float32), low.astype(jnp.float32)).astype(jnp.bfloat16)


def dot_exact(a, b):
    return jnp.dot(a, b, precision=EXACT, preferred_element_type=jnp.float32)


def dot_half(a, b):
    return jnp.dot(a, b, preferred_element_type=jnp.float32)


def ordered_parts(lines, plain, order, halves):
    rows, lats = lines.shape[1:]
    for side in range(PAIR):
        high, low = halve(lines[side])
        plain[2 * side * rows : (2 * side + 1) * rows, :] = high
        plain[(2 * side + 1) * rows : (2 * side + 2) * rows, :] = low
    ordered = dot_half(plain[...], order[...])
    for side in range(PAIR):
        place = slice(side * lats, (side + 1) * lats)
        both = ordered[2 * side * rows : 2 * (side + 1) * rows].astype(jnp.bfloat16)
        halves[0 : 2 * rows, place] = both
        halves[2 * rows : 3 * rows, place] = both[0:rows]


def plane(lons, lon, var):
    side, at = divmod(lon, lons // 2)
    group, place = divmod(at, PAIR)
    if side == 0:
        return 3 * PAIR * group + place if var == 0 else None
    return 3 * PAIR * group + PAIR + 2 * place + var


def mix_kernel(shape, offsets, at, *refs):
    levels, own, padded, lons, tiles, targets = shape
    (gradient, bal, cor_a, cor_b, order), refs = refs[:5], refs[5:]
    outs, (weight, weight_raw, lines, plain, halves, grads, sems) = refs[:-7], refs[-7:]
    lats = tiles * LANES
    step = pl.program_id(0)

    @pl.when(step == 0)
    def _():
        arriving = [
            pltpu.make_async_copy(gradient.at[:, lane_tile(j)], grads.at[j], sems.at[j]) for j in range(tiles)
        ]
        for copy in arriving:
            copy.start()
        first = [at[0], None] * 3
        second = [None, at[0]] * 3
        take_first = pick_levels(6 * padded, levels, padded, own, first)
        take_second = pick_levels(6 * padded, levels, padded, own, second)
        pick = pick_levels(targets * padded, levels, padded, own, [at[t] for t in range(targets)])
        cols_a = dot_t(pick, cor_a[...])
        through_a = dot_t(cols_a, take_first + dot_exact(take_second, bal[...]))
        through_b = dot_t(dot_t(pick, cor_b[...]), take_second)
        only_first = dot_t(cols_a, take_first)
        weight[...] = three_parts(jnp.concatenate([through_a, through_b], 0), 2 * padded)
        weight_raw[...] = three_parts(
            jnp.concatenate([through_a[:padded], only_first[padded:], through_b[:padded]], 0), 2 * padded
        )
        lines[...] = jnp.zeros_like(lines)
        for copy in arriving:
            copy.wait()

    for half in range(2):
        for side in range(PAIR):
            lon = half * (lons // 2) + step * PAIR + side
            for var in range(2):
                for j in range(tiles):
                    lines[half, side, pl.ds(var * padded, own), lane_tile(j)] = grads[
                        j, pl.ds(var * lons + lon, own, stride=2 * lons), :
                    ]
        ordered_parts(lines.at[half], plain.at[half], order, halves.at[half])
    for half in range(2):
        mixed = dot_half((weight_raw if half == 0 else weight)[...], halves[half])
        for side in range(PAIR):
            place = slice(side * lats, (side + 1) * lats)
            for target in range(targets):
                for var in range(2):
                    if half == 0 and target > 0 and var == 1:
                        continue
                    first = (var * targets + target) * padded
                    for c, (start, size) in enumerate(offsets):
                        out = outs[target * len(offsets) + c]
                        value = mixed[first + start : first + start + size, place]
                        if target == 0:
                            out[half, side, var] = value
                        else:
                            out[plane(lons, half * (lons // 2) + side, var)] = value


def raw_kernel(shape, offsets, at, *refs):
    levels, own, padded, lons, tiles, targets = shape
    chunks = len(offsets)
    raws, refs = refs[: tiles * (targets - 1)], refs[tiles * (targets - 1) :]
    (bal, cor_a, cor_b, order), kept, outs = refs[:4], refs[4 : 4 + chunks], refs[4 + chunks : 4 + 2 * chunks]
    weight, lines, plain, halves = refs[4 + 2 * chunks :]
    lats = tiles * LANES
    step = pl.program_id(0)

    @pl.when(step == 0)
    def _():
        pick = pick_levels(padded, levels, padded, own, [at[0]])
        cols_a = dot_t(pick, cor_a[...])
        cols_b = dot_t(pick, cor_b[...])
        for source in range(1, targets):
            take = pick_levels(3 * padded, levels, padded, own, [at[source]] * 3)
            full = jnp.concatenate([dot_t(cols_a, dot_exact(take, bal[...])), dot_t(cols_b, take)], 0)
            weight[source - 1] = three_parts(full, padded)
        lines[...] = jnp.zeros_like(lines)

    total = None
    for source in range(targets - 1):
        for side in range(PAIR):
            for j in range(tiles):
                lines[side, 0:own, lane_tile(j)] = raws[source * tiles + j][
                    pl.ds(step * PAIR + side, own, stride=lons // 2), :
                ]
        ordered_parts(lines, plain, order, halves)
        mixed = dot_half(weight[source], halves[...])
        total = mixed if total is None else total + mixed
    for side in range(PAIR):
        place = slice(side * lats, (side + 1) * lats)
        for var in range(2):
            for (start, size), more, out in zip(offsets, kept, outs):
                first = var * padded + start
                out[0, side, var] = more[0, side, var] + total[first : first + size, place]


def coef_kernel(own, padded, lons, halo, tiles, sea, rough, order, _, coef, first, last, seas, roughs, lines, values, sems):
    arriving = []
    for j in range(tiles):
        for source, held in ((sea, seas), (rough, roughs)):
            arriving.append(pltpu.make_async_copy(source.at[:, lane_tile(j)], held.at[j], sems.at[len(arriving)]))
    for copy in arriving:
        copy.start()
    lines[...] = jnp.zeros_like(lines)
    for copy in arriving:
        copy.wait()
    size = lons // COEF_GROUPS
    leaving = []

    def leave(source, target):
        copy = pltpu.make_async_copy(source, target, sems.at[len(arriving) + len(leaving)])
        copy.start()
        leaving.append(copy)

    for group in range(COEF_GROUPS):
        for at in range(size):
            rows = pl.ds(group * size + at, own, stride=lons)
            for j in range(tiles):
                lines[at * padded : at * padded + own, lane_tile(j)] = (
                    seas[j, rows, :].astype(jnp.float32) * roughs[j, rows, :]
                )
        high, low = halve(lines[...])
        value = dot_half(high, order[...]) + dot_half(low, order[...])
        for at in range(size):
            values[group * size + at] = value[at * padded : (at + 1) * padded]
        start, stop = group * size, (group + 1) * size
        leave(values.at[start:stop], coef.at[start:stop])
        if start < halo:
            until = min(stop, halo)
            leave(values.at[start:until], first.at[start:until])
        if stop > lons - halo:
            since = max(start, lons - halo)
            leave(values.at[since:stop], last.at[since - (lons - halo) : stop - (lons - halo)])
    for copy in leaving:
        copy.wait()


def mixed_at(lons, sums, lon, var):
    value = sums[0][lon // (lons // 2), lon % (lons // 2), var]
    at = plane(lons, lon, var)
    if at is not None:
        for more in sums[1:]:
            value = value + more[at]
    return value


def edge_kernel(lons, halo, parts, passed, *refs):
    sums, coef, (first, last, token) = refs[:parts], refs[parts], refs[parts + 4 + passed : parts + 7 + passed]
    token[...] = jnp.zeros_like(token)
    for lon in range(lons):
        for var in range(2):
            value = coef[lon] * mixed_at(lons, sums, lon, var)
            if lon < halo:
                first[lon, var] = value
            if lon >= lons - halo:
                last[lon - (lons - halo), var] = value


def neighbours(tiles, lane):
    count = len(tiles)
    before = jnp.where(lane == 0, tiles[0], pltpu.roll(tiles[-1], 1, 1))
    after = jnp.where(lane == LANES - 1, tiles[-1], pltpu.roll(tiles[0], LANES - 1, 1))
    line = [before, *tiles, after]
    return [line[j] + line[j + 2] for j in range(count)]


def diffuse(lons, lats, sums, coef, before, after, coef_before, coef_after, rates, weighted, square):
    halo = PASSES
    tiles = lats // LANES
    lane = lax.broadcasted_iota(jnp.int32, (ROWS, LANES), 1)

    for lon in range(lons):
        scale = coef[lon]
        square[halo + lon] = scale * scale
        for var in range(2):
            weighted[0][halo + lon, var] = scale * mixed_at(lons, sums, lon, var)
    for lon in range(halo):
        weighted[0][lon] = before[lon]
        weighted[0][halo + lons + lon] = after[lon]
    for lon in range(halo - 1):
        square[1 + lon] = coef_before[lon] * coef_before[lon]
        square[halo + lons + lon] = coef_after[lon] * coef_after[lon]

    for section in range(PASSES):
        source, target = weighted[section % 2], weighted[(section + 1) % 2]
        rate = rates[section]
        start = section + 1
        stop = lons + 2 * halo - 1 - section

        def one_variable(var, carry):
            def load(lon):
                return [source[lon, var, :, lane_tile(j)] for j in range(tiles)]

            behind, here = load(start - 1), load(start)
            for lon in range(start, stop):
                ahead = load(lon + 1)
                lat = neighbours(here, lane)
                for j in range(tiles):
                    factor = rate * square[lon, :, lane_tile(j)]
                    spread = (behind[j] + ahead[j]) + lat[j] - 4.0 * here[j]
                    target[lon, var, :, lane_tile(j)] = here[j] + factor * spread
                behind, here = here, ahead
            return carry

        lax.fori_loop(0, 2, one_variable, 0)


def diffuse_kernel(lons, lats, parts, *refs):
    sums, rest = refs[:parts], refs[parts:]
    coef, before, after, coef_before, coef_after, rates, back, _, _, out, token, *rest = rest
    *weighted, square, lines = rest
    tiles = lats // LANES
    token[...] = jnp.zeros_like(token)
    diffuse(lons, lats, sums, coef, before, after, coef_before, coef_after, rates, weighted, square)

    count = ROWS * 2 * lons
    for lon in range(lons):
        scale = coef[lon]
        land = scale == 0.0
        inverse = 1.0 / jnp.where(land, 1.0, scale)
        for var in range(2):
            plain = mixed_at(lons, sums, lon, var)
            value = jnp.where(land, plain, weighted[PASSES % 2][PASSES + lon, var] * inverse)
            for j in range(tiles):
                lines[pl.ds(j * count + var * lons + lon, ROWS, stride=2 * lons), :] = value[:, lane_tile(j)]
    high, low = halve(jnp.concatenate([lines[j * count : (j + 1) * count, :] for j in range(tiles)], 1))
    out[...] = jnp.dot(high, back[...], preferred_element_type=jnp.float32) + jnp.dot(
        low, back[...], preferred_element_type=jnp.float32
    )


def whole(*block):
    return pl.BlockSpec(block, lambda i: (0,) * len(block))


def params():
    return pltpu.CompilerParams(vmem_limit_bytes=VMEM_LIMIT)


def spent(microseconds):
    return pl.CostEstimate(flops=int(microseconds * 1.153e9), bytes_accessed=1024, transcendentals=0)


def on_device(gradient, land_sea, roughness, scale_index, scale_table, balance, corr_a, corr_b):
    own, _, lons, lats = gradient.shape
    levels = balance.shape[0]
    lev_count = lax.axis_size("lev")
    tile_count = lax.axis_size("tile")
    me = lax.axis_index("lev")
    units = -(-own // ROWS)
    padded = units * ROWS
    chunks = chunk_units(units)
    starts = [sum(chunks[:c]) for c in range(len(chunks))]
    offsets = [(s * ROWS, c * ROWS) for s, c in zip(starts, chunks)]
    halo = PASSES
    unit_bytes = lons * 2 * ROWS * lats * 4
    f32 = jnp.float32
    hidden = pl.BlockSpec(memory_space=pl.ANY)

    def along(shift):
        return [(i, (i + shift) % lev_count) for i in range(lev_count)]

    with jax.named_scope("raw"):
        rows = gradient[:, 1, : lons // 2]
        raws = [lax.ppermute(rows, "lev", along(shift)) for shift in range(1, lev_count)]

    tiles = lats // LANES
    place = np.arange(lats)
    order = np.zeros((lats, lats), np.float32)
    order[place, (place % tiles) * LANES + place // tiles] = 1.0
    back = jnp.asarray(order.T, jnp.bfloat16)
    order = jnp.asarray(order, jnp.bfloat16)

    up = [(i, (i + 1) % tile_count) for i in range(tile_count)]
    down = [(j, i) for i, j in up]
    with jax.named_scope("coef"):
        coef, first, last = pl.pallas_call(
            functools.partial(coef_kernel, own, padded, lons, halo - 1, tiles),
            out_shape=[
                jax.ShapeDtypeStruct((lons, padded, lats), f32),
                jax.ShapeDtypeStruct((halo - 1, padded, lats), f32),
                jax.ShapeDtypeStruct((halo - 1, padded, lats), f32),
            ],
            in_specs=[hidden, hidden, pl.BlockSpec(memory_space=pltpu.VMEM), hidden],
            out_specs=[hidden] * 3,
            scratch_shapes=[
                pltpu.VMEM((tiles, own * lons, LANES), jnp.int32),
                pltpu.VMEM((tiles, own * lons, LANES), f32),
                pltpu.VMEM((lons // COEF_GROUPS * padded, lats), f32),
                pltpu.VMEM((lons, padded, lats), f32),
                pltpu.SemaphoreType.DMA((2 * tiles + 3 * COEF_GROUPS,)),
            ],
            compiler_params=params(),
            cost_estimate=spent(10),
            name="coef",
        )(land_sea.reshape(own * lons, lats), roughness.reshape(own * lons, lats), order, rows)
        coef_before = lax.ppermute(last, "tile", up)
        coef_after = lax.ppermute(first, "tile", down)

    half = lons // 2
    shape = (levels, own, padded, lons, tiles, lev_count)
    kept_shapes = [jax.ShapeDtypeStruct((2, half, 2, size, lats), f32) for _, size in offsets]
    sent_shapes = [jax.ShapeDtypeStruct((3 * half, size, lats), f32) for _, size in offsets]
    kept_specs = [pl.BlockSpec((2, PAIR, 2, size, lats), lambda i: (0, i, 0, 0, 0)) for _, size in offsets]
    sent_specs = [pl.BlockSpec((3 * PAIR, size, lats), lambda i: (i, 0, 0)) for _, size in offsets]
    level_starts = [lax.rem(me + shift, lev_count) * own for shift in range(lev_count)]
    with jax.named_scope("mix"):
        mixed = pl.pallas_call(
            functools.partial(mix_kernel, shape, offsets),
            grid=(half // PAIR,),
            out_shape=kept_shapes + sent_shapes * (lev_count - 1),
            in_specs=[pl.BlockSpec(memory_space=pltpu.SMEM)]
            + [hidden]
            + [whole(levels, levels)] * 3
            + [whole(lats, lats)],
            out_specs=kept_specs + sent_specs * (lev_count - 1),
            scratch_shapes=[
                pltpu.VMEM((2 * lev_count * padded, 6 * padded), jnp.bfloat16),
                pltpu.VMEM(((lev_count + 1) * padded, 6 * padded), jnp.bfloat16),
                pltpu.VMEM((2, PAIR, 2 * padded, lats), f32),
                pltpu.VMEM((2, PAIR * 4 * padded, lats), jnp.bfloat16),
                pltpu.VMEM((2, 6 * padded, PAIR * lats), jnp.bfloat16),
                pltpu.VMEM((tiles, own * 2 * lons, LANES), f32),
                pltpu.SemaphoreType.DMA((tiles,)),
            ],
            compiler_params=params(),
            cost_estimate=spent(20),
            name="mix",
        )(
            jnp.stack(level_starts),
            gradient.reshape(own * 2 * lons, lats),
            balance,
            corr_a,
            corr_b,
            order,
        )
        sent = [mixed[c + len(chunks) :: len(chunks)] for c in range(len(chunks))]

        def send(arrays):
            return [lax.ppermute(array, "lev", along(shift + 1)) for shift, array in enumerate(arrays)]

        final = len(chunks) - 1
        received = [send(arrays) if c < final or final < 2 else None for c, arrays in enumerate(sent)]

    with jax.named_scope("raw"):
        kept = pl.pallas_call(
            functools.partial(raw_kernel, shape, offsets),
            grid=(half // PAIR,),
            out_shape=kept_shapes,
            in_specs=[pl.BlockSpec(memory_space=pltpu.SMEM)]
            + [pl.BlockSpec((own * half, LANES), lambda i, j=j: (0, j)) for j in range(tiles)] * (lev_count - 1)
            + [whole(levels, levels)] * 3
            + [whole(lats, lats)]
            + [pl.BlockSpec((1, PAIR, 2, size, lats), lambda i: (0, i, 0, 0, 0)) for _, size in offsets],
            out_specs=[pl.BlockSpec((1, PAIR, 2, size, lats), lambda i: (0, i, 0, 0, 0)) for _, size in offsets],
            scratch_shapes=[
                pltpu.VMEM((lev_count - 1, 2 * padded, 3 * padded), jnp.bfloat16),
                pltpu.VMEM((PAIR, padded, lats), f32),
                pltpu.VMEM((PAIR * 2 * padded, lats), jnp.bfloat16),
                pltpu.VMEM((3 * padded, PAIR * lats), jnp.bfloat16),
            ],
            input_output_aliases={5 + tiles * (lev_count - 1) + c: c for c in range(len(chunks))},
            compiler_params=params(),
            cost_estimate=spent(6),
            name="raw",
        )(
            jnp.stack([level_starts[(lev_count - shift) % lev_count] for shift in range(lev_count)]),
            *[part for raw in raws for part in [raw.reshape(own * half, lats)] * tiles],
            balance,
            corr_a,
            corr_b,
            order,
            *mixed[: len(chunks)],
        )

    with jax.named_scope("rates"):
        own_index = lax.dynamic_slice_in_dim(scale_index, me * own, own, 1)
        picks = own_index[:, :, None] == jnp.arange(NSCALE, dtype=jnp.int32)[None, None, :]
        rates = jnp.sum(picks.astype(f32) * scale_table[None, None, :], -1)
        rates = jnp.pad(rates, ((0, 0), (0, padded - own)))
        rates = jnp.broadcast_to(rates[:, :, None], (PASSES, padded, LANES))

    token_shape = jax.ShapeDtypeStruct((ROWS, LANES), f32)
    token_spec = pl.BlockSpec((ROWS, LANES), lambda i: (0, 0))
    result = jnp.zeros((ROWS, LANES), f32)
    token = result

    def sum_specs(parts):
        own_sum = pl.BlockSpec((2, half, 2, ROWS, lats), lambda i: (0, 0, 0, i, 0))
        return [own_sum] + [pl.BlockSpec((3 * half, ROWS, lats), lambda i: (0, i, 0))] * (parts - 1)

    def edges(c, token, passed):
        sums = [kept[c]] + received[c]
        count, start = chunks[c], starts[c]
        halo_shape = jax.ShapeDtypeStruct((halo, 2, count * ROWS, lats), f32)
        fixed = [jax.ShapeDtypeStruct(array.shape, array.dtype) for array in passed]
        with jax.named_scope("edges"):
            first, last, token, *passed = pl.pallas_call(
                functools.partial(edge_kernel, lons, halo, len(sums), len(passed)),
                grid=(count,),
                out_shape=[halo_shape, halo_shape, token_shape, *fixed],
                in_specs=sum_specs(len(sums))
                + [pl.BlockSpec((lons, ROWS, lats), lambda i: (0, start + i, 0))]
                + [hidden] * (3 + len(passed)),
                out_specs=[pl.BlockSpec((halo, 2, ROWS, lats), lambda i: (0, 0, i, 0))] * 2
                + [token_spec]
                + [hidden] * len(passed),
                input_output_aliases={len(sums) + 4 + i: 3 + i for i in range(len(passed))},
                compiler_params=params(),
                cost_estimate=spent(2),
                name="edges",
            )(*sums, coef, coef_before, coef_after, token, *passed)
            return lax.ppermute(last, "tile", up), lax.ppermute(first, "tile", down), token, passed

    def diffusion(c, before, after, result, token):
        sums = [kept[c]] + received[c]
        count, start = chunks[c], starts[c]
        fixed = lambda i: (0, 0, i, 0)
        level = lambda i: (0, start + i, 0)
        operands = [*sums, coef, before, after, coef_before, coef_after, rates, back, token, result]
        with jax.named_scope("diffusion"):
            return pl.pallas_call(
                functools.partial(diffuse_kernel, lons, lats, len(sums)),
                grid=(count,),
                out_shape=[jax.ShapeDtypeStruct((own * 2 * lons, lats), f32), token_shape],
                in_specs=sum_specs(len(sums))
                + [pl.BlockSpec((lons, ROWS, lats), level)]
                + [pl.BlockSpec((halo, 2, ROWS, lats), fixed)] * 2
                + [pl.BlockSpec((halo - 1, ROWS, lats), level)] * 2
                + [pl.BlockSpec((PASSES, ROWS, LANES), level), whole(lats, lats), hidden, hidden],
                out_specs=[pl.BlockSpec((ROWS * 2 * lons, lats), lambda i: (start + i, 0)), token_spec],
                scratch_shapes=[
                    pltpu.VMEM((lons + 2 * halo, 2, ROWS, lats), f32),
                    pltpu.VMEM((lons + 2 * halo, 2, ROWS, lats), f32),
                    pltpu.VMEM((lons + 2 * halo, ROWS, lats), f32),
                    pltpu.VMEM((tiles * ROWS * 2 * lons, LANES), f32),
                ],
                input_output_aliases={} if c == 0 else {len(operands) - 1: 0},
                compiler_params=params(),
                cost_estimate=spent(11),
                name="diffusion",
            )(*operands)

    waiting = None
    for c in range(len(chunks)):
        before, after, token, passed = edges(c, token, sent[final] if c == final - 2 else [])
        if c == final - 2:
            received[final] = send(passed)
        if waiting is not None:
            result, token = diffusion(c - 1, *waiting, result, token)
        waiting = (before, after)
    result, _ = diffusion(len(chunks) - 1, *waiting, result, token)
    return result.reshape(own, 2, lons, lats)


def solution(mesh):
    return jax.shard_map(
        on_device,
        mesh=mesh,
        in_specs=(
            P("lev", None, "tile", None),
            P("lev", "tile", None),
            P("lev", "tile", None),
            P(),
            P(),
            P(),
            P(),
            P(),
        ),
        out_specs=P("lev", None, "tile", None),
        check_vma=False,
    )
```

```python
import functools

import jax
import jax.numpy as jnp
import numpy as np
from jax import lax
from jax.experimental import pallas as pl
from jax.experimental.pallas import tpu as pltpu
from jax.sharding import PartitionSpec as P

PASSES = 10
NSCALE = 8
ROWS = 8
LANES = 128
COEF_GROUPS = 4
PAIR = 2
EXACT = lax.Precision.HIGHEST


def chunk_units(total):
    return [2] * (total // 2) + [1] * (total % 2)


def lane_tile(j):
    return slice(j * LANES, (j + 1) * LANES)


def dot_t(a, b):
    return lax.dot_general(
        a, b, (((1,), (1,)), ((), ())), precision=EXACT, preferred_element_type=jnp.float32
    )


def halve(value):
    high = value.astype(jnp.bfloat16)
    return high, (value - high.astype(jnp.float32)).astype(jnp.bfloat16)


def pick_levels(rows, levels, padded, own, starts):
    row = lax.broadcasted_iota(jnp.int32, (rows, levels), 0)
    col = lax.broadcasted_iota(jnp.int32, (rows, levels), 1)
    picked = jnp.zeros((rows, levels), jnp.bool_)
    for s, start in enumerate(starts):
        if start is not None:
            at = row - s * padded
            picked = picked | ((at >= 0) & (at < own) & (col == at + start))
    return picked.astype(jnp.float32)


def three_parts(full, third):
    high, low = halve(full)
    part = lax.broadcasted_iota(jnp.int32, full.shape, 1)
    return jnp.where(part < 2 * third, high.astype(jnp.float32), low.astype(jnp.float32)).astype(jnp.bfloat16)


def dot_exact(a, b):
    return jnp.dot(a, b, precision=EXACT, preferred_element_type=jnp.float32)


def dot_half(a, b):
    return jnp.dot(a, b, preferred_element_type=jnp.float32)


def ordered_parts(lines, plain, order, halves):
    rows, lats = lines.shape[1:]
    for side in range(PAIR):
        high, low = halve(lines[side])
        plain[2 * side * rows : (2 * side + 1) * rows, :] = high
        plain[(2 * side + 1) * rows : (2 * side + 2) * rows, :] = low
    ordered = dot_half(plain[...], order[...])
    for side in range(PAIR):
        place = slice(side * lats, (side + 1) * lats)
        both = ordered[2 * side * rows : 2 * (side + 1) * rows].astype(jnp.bfloat16)
        halves[0 : 2 * rows, place] = both
        halves[2 * rows : 3 * rows, place] = both[0:rows]


def plane(lons, lon, var):
    side, at = divmod(lon, lons // 2)
    group, place = divmod(at, PAIR)
    if side == 0:
        return 3 * PAIR * group + place if var == 0 else None
    return 3 * PAIR * group + PAIR + 2 * place + var


def mix_kernel(shape, offsets, at, *refs):
    levels, own, padded, lons, tiles, targets = shape
    (gradient, bal, cor_a, cor_b, order), refs = refs[:5], refs[5:]
    outs, (weight, weight_raw, lines, plain, halves, grads, sems) = refs[:-7], refs[-7:]
    lats = tiles * LANES
    step = pl.program_id(0)

    @pl.when(step == 0)
    def _():
        arriving = [
            pltpu.make_async_copy(gradient.at[:, lane_tile(j)], grads.at[j], sems.at[j]) for j in range(tiles)
        ]
        for copy in arriving:
            copy.start()
        first = [at[0], None] * 3
        second = [None, at[0]] * 3
        take_first = pick_levels(6 * padded, levels, padded, own, first)
        take_second = pick_levels(6 * padded, levels, padded, own, second)
        pick = pick_levels(targets * padded, levels, padded, own, [at[t] for t in range(targets)])
        cols_a = dot_t(pick, cor_a[...])
        through_a = dot_t(cols_a, take_first + dot_exact(take_second, bal[...]))
        through_b = dot_t(dot_t(pick, cor_b[...]), take_second)
        only_first = dot_t(cols_a, take_first)
        weight[...] = three_parts(jnp.concatenate([through_a, through_b], 0), 2 * padded)
        weight_raw[...] = three_parts(
            jnp.concatenate([through_a[:padded], only_first[padded:], through_b[:padded]], 0), 2 * padded
        )
        lines[...] = jnp.zeros_like(lines)
        for copy in arriving:
            copy.wait()

    for half in range(2):
        for side in range(PAIR):
            lon = half * (lons // 2) + step * PAIR + side
            for var in range(2):
                for j in range(tiles):
                    lines[half, side, pl.ds(var * padded, own), lane_tile(j)] = grads[
                        j, pl.ds(var * lons + lon, own, stride=2 * lons), :
                    ]
        ordered_parts(lines.at[half], plain.at[half], order, halves.at[half])
    for half in range(2):
        mixed = dot_half((weight_raw if half == 0 else weight)[...], halves[half])
        for side in range(PAIR):
            place = slice(side * lats, (side + 1) * lats)
            for target in range(targets):
                for var in range(2):
                    if half == 0 and target > 0 and var == 1:
                        continue
                    first = (var * targets + target) * padded
                    for c, (start, size) in enumerate(offsets):
                        out = outs[target * len(offsets) + c]
                        value = mixed[first + start : first + start + size, place]
                        if target == 0:
                            out[half, side, var] = value
                        else:
                            out[plane(lons, half * (lons // 2) + side, var)] = value


def raw_kernel(shape, offsets, at, *refs):
    levels, own, padded, lons, tiles, targets = shape
    chunks = len(offsets)
    raws, refs = refs[: tiles * (targets - 1)], refs[tiles * (targets - 1) :]
    (bal, cor_a, cor_b, order), kept, outs = refs[:4], refs[4 : 4 + chunks], refs[4 + chunks : 4 + 2 * chunks]
    weight, lines, plain, halves = refs[4 + 2 * chunks :]
    lats = tiles * LANES
    step = pl.program_id(0)

    @pl.when(step == 0)
    def _():
        pick = pick_levels(padded, levels, padded, own, [at[0]])
        cols_a = dot_t(pick, cor_a[...])
        cols_b = dot_t(pick, cor_b[...])
        for source in range(1, targets):
            take = pick_levels(3 * padded, levels, padded, own, [at[source]] * 3)
            full = jnp.concatenate([dot_t(cols_a, dot_exact(take, bal[...])), dot_t(cols_b, take)], 0)
            weight[source - 1] = three_parts(full, padded)
        lines[...] = jnp.zeros_like(lines)

    total = None
    for source in range(targets - 1):
        for side in range(PAIR):
            for j in range(tiles):
                lines[side, 0:own, lane_tile(j)] = raws[source * tiles + j][
                    pl.ds(step * PAIR + side, own, stride=lons // 2), :
                ]
        ordered_parts(lines, plain, order, halves)
        mixed = dot_half(weight[source], halves[...])
        total = mixed if total is None else total + mixed
    for side in range(PAIR):
        place = slice(side * lats, (side + 1) * lats)
        for var in range(2):
            for (start, size), more, out in zip(offsets, kept, outs):
                first = var * padded + start
                out[0, side, var] = more[0, side, var] + total[first : first + size, place]


def coef_kernel(own, padded, lons, halo, tiles, sea, rough, order, _, coef, first, last, seas, roughs, lines, values, sems):
    arriving = []
    for j in range(tiles):
        for source, held in ((sea, seas), (rough, roughs)):
            arriving.append(pltpu.make_async_copy(source.at[:, lane_tile(j)], held.at[j], sems.at[len(arriving)]))
    for copy in arriving:
        copy.start()
    lines[...] = jnp.zeros_like(lines)
    for copy in arriving:
        copy.wait()
    size = lons // COEF_GROUPS
    leaving = []

    def leave(source, target):
        copy = pltpu.make_async_copy(source, target, sems.at[len(arriving) + len(leaving)])
        copy.start()
        leaving.append(copy)

    for group in range(COEF_GROUPS):
        for at in range(size):
            rows = pl.ds(group * size + at, own, stride=lons)
            for j in range(tiles):
                lines[at * padded : at * padded + own, lane_tile(j)] = (
                    seas[j, rows, :].astype(jnp.float32) * roughs[j, rows, :]
                )
        high, low = halve(lines[...])
        value = dot_half(high, order[...]) + dot_half(low, order[...])
        for at in range(size):
            values[group * size + at] = value[at * padded : (at + 1) * padded]
        start, stop = group * size, (group + 1) * size
        leave(values.at[start:stop], coef.at[start:stop])
        if start < halo:
            until = min(stop, halo)
            leave(values.at[start:until], first.at[start:until])
        if stop > lons - halo:
            since = max(start, lons - halo)
            leave(values.at[since:stop], last.at[since - (lons - halo) : stop - (lons - halo)])
    for copy in leaving:
        copy.wait()


def mixed_at(lons, sums, lon, var):
    value = sums[0][lon // (lons // 2), lon % (lons // 2), var]
    at = plane(lons, lon, var)
    if at is not None:
        for more in sums[1:]:
            value = value + more[at]
    return value


def edge_kernel(lons, halo, parts, passed, *refs):
    sums, coef, (first, last, token) = refs[:parts], refs[parts], refs[parts + 4 + passed : parts + 7 + passed]
    token[...] = jnp.zeros_like(token)
    for lon in range(lons):
        for var in range(2):
            value = coef[lon] * mixed_at(lons, sums, lon, var)
            if lon < halo:
                first[lon, var] = value
            if lon >= lons - halo:
                last[lon - (lons - halo), var] = value


def neighbours(tiles, lane):
    count = len(tiles)
    before = jnp.where(lane == 0, tiles[0], pltpu.roll(tiles[-1], 1, 1))
    after = jnp.where(lane == LANES - 1, tiles[-1], pltpu.roll(tiles[0], LANES - 1, 1))
    line = [before, *tiles, after]
    return [line[j] + line[j + 2] for j in range(count)]


def diffuse(lons, lats, sums, coef, before, after, coef_before, coef_after, rates, weighted, square):
    halo = PASSES
    tiles = lats // LANES
    lane = lax.broadcasted_iota(jnp.int32, (ROWS, LANES), 1)

    for lon in range(lons):
        scale = coef[lon]
        square[halo + lon] = scale * scale
        for var in range(2):
            weighted[0][halo + lon, var] = scale * mixed_at(lons, sums, lon, var)
    for lon in range(halo):
        weighted[0][lon] = before[lon]
        weighted[0][halo + lons + lon] = after[lon]
    for lon in range(halo - 1):
        square[1 + lon] = coef_before[lon] * coef_before[lon]
        square[halo + lons + lon] = coef_after[lon] * coef_after[lon]

    for section in range(PASSES):
        source, target = weighted[section % 2], weighted[(section + 1) % 2]
        rate = rates[section]
        start = section + 1
        stop = lons + 2 * halo - 1 - section

        def one_variable(var, carry):
            def load(lon):
                return [source[lon, var, :, lane_tile(j)] for j in range(tiles)]

            behind, here = load(start - 1), load(start)
            for lon in range(start, stop):
                ahead = load(lon + 1)
                lat = neighbours(here, lane)
                for j in range(tiles):
                    factor = rate * square[lon, :, lane_tile(j)]
                    spread = (behind[j] + ahead[j]) + lat[j] - 4.0 * here[j]
                    target[lon, var, :, lane_tile(j)] = here[j] + factor * spread
                behind, here = here, ahead
            return carry

        lax.fori_loop(0, 2, one_variable, 0)


def diffuse_kernel(lons, lats, parts, *refs):
    sums, rest = refs[:parts], refs[parts:]
    coef, before, after, coef_before, coef_after, rates, back, _, _, out, token, *rest = rest
    *weighted, square, lines = rest
    tiles = lats // LANES
    token[...] = jnp.zeros_like(token)
    diffuse(lons, lats, sums, coef, before, after, coef_before, coef_after, rates, weighted, square)

    count = ROWS * 2 * lons
    for lon in range(lons):
        scale = coef[lon]
        land = scale == 0.0
        inverse = 1.0 / jnp.where(land, 1.0, scale)
        for var in range(2):
            plain = mixed_at(lons, sums, lon, var)
            value = jnp.where(land, plain, weighted[PASSES % 2][PASSES + lon, var] * inverse)
            for j in range(tiles):
                lines[pl.ds(j * count + var * lons + lon, ROWS, stride=2 * lons), :] = value[:, lane_tile(j)]
    high, low = halve(jnp.concatenate([lines[j * count : (j + 1) * count, :] for j in range(tiles)], 1))
    out[...] = jnp.dot(high, back[...], preferred_element_type=jnp.float32) + jnp.dot(
        low, back[...], preferred_element_type=jnp.float32
    )


def whole(*block):
    return pl.BlockSpec(block, lambda i: (0,) * len(block))


def params(mebibytes):
    return pltpu.CompilerParams(vmem_limit_bytes=mebibytes * 1024 * 1024)


def spent(microseconds):
    return pl.CostEstimate(flops=int(microseconds * 1.153e9), bytes_accessed=1024, transcendentals=0)


def on_device(gradient, land_sea, roughness, scale_index, scale_table, balance, corr_a, corr_b):
    own, _, lons, lats = gradient.shape
    levels = balance.shape[0]
    lev_count = lax.axis_size("lev")
    tile_count = lax.axis_size("tile")
    me = lax.axis_index("lev")
    units = -(-own // ROWS)
    padded = units * ROWS
    chunks = chunk_units(units)
    starts = [sum(chunks[:c]) for c in range(len(chunks))]
    offsets = [(s * ROWS, c * ROWS) for s, c in zip(starts, chunks)]
    halo = PASSES
    unit_bytes = lons * 2 * ROWS * lats * 4
    f32 = jnp.float32
    hidden = pl.BlockSpec(memory_space=pl.ANY)

    def along(shift):
        return [(i, (i + shift) % lev_count) for i in range(lev_count)]

    with jax.named_scope("raw"):
        rows = gradient[:, 1, : lons // 2]
        raws = [lax.ppermute(rows, "lev", along(shift)) for shift in range(1, lev_count)]

    tiles = lats // LANES
    place = np.arange(lats)
    order = np.zeros((lats, lats), np.float32)
    order[place, (place % tiles) * LANES + place // tiles] = 1.0
    back = jnp.asarray(order.T, jnp.bfloat16)
    order = jnp.asarray(order, jnp.bfloat16)

    up = [(i, (i + 1) % tile_count) for i in range(tile_count)]
    down = [(j, i) for i, j in up]
    with jax.named_scope("coef"):
        coef, first, last = pl.pallas_call(
            functools.partial(coef_kernel, own, padded, lons, halo - 1, tiles),
            out_shape=[
                jax.ShapeDtypeStruct((lons, padded, lats), f32),
                jax.ShapeDtypeStruct((halo - 1, padded, lats), f32),
                jax.ShapeDtypeStruct((halo - 1, padded, lats), f32),
            ],
            in_specs=[hidden, hidden, pl.BlockSpec(memory_space=pltpu.VMEM), hidden],
            out_specs=[hidden] * 3,
            scratch_shapes=[
                pltpu.VMEM((tiles, own * lons, LANES), jnp.int32),
                pltpu.VMEM((tiles, own * lons, LANES), f32),
                pltpu.VMEM((lons // COEF_GROUPS * padded, lats), f32),
                pltpu.VMEM((lons, padded, lats), f32),
                pltpu.SemaphoreType.DMA((2 * tiles + 3 * COEF_GROUPS,)),
            ],
            compiler_params=params(53),
            cost_estimate=spent(10),
            name="coef",
        )(land_sea.reshape(own * lons, lats), roughness.reshape(own * lons, lats), order, rows)
        coef_before = lax.ppermute(last, "tile", up)
        coef_after = lax.ppermute(first, "tile", down)

    half = lons // 2
    shape = (levels, own, padded, lons, tiles, lev_count)
    kept_shapes = [jax.ShapeDtypeStruct((2, half, 2, size, lats), f32) for _, size in offsets]
    sent_shapes = [jax.ShapeDtypeStruct((3 * half, size, lats), f32) for _, size in offsets]
    kept_specs = [pl.BlockSpec((2, PAIR, 2, size, lats), lambda i: (0, i, 0, 0, 0)) for _, size in offsets]
    sent_specs = [pl.BlockSpec((3 * PAIR, size, lats), lambda i: (i, 0, 0)) for _, size in offsets]
    level_starts = [lax.rem(me + shift, lev_count) * own for shift in range(lev_count)]
    with jax.named_scope("mix"):
        mixed = pl.pallas_call(
            functools.partial(mix_kernel, shape, offsets),
            grid=(half // PAIR,),
            out_shape=kept_shapes + sent_shapes * (lev_count - 1),
            in_specs=[pl.BlockSpec(memory_space=pltpu.SMEM)]
            + [hidden]
            + [whole(levels, levels)] * 3
            + [whole(lats, lats)],
            out_specs=kept_specs + sent_specs * (lev_count - 1),
            scratch_shapes=[
                pltpu.VMEM((2 * lev_count * padded, 6 * padded), jnp.bfloat16),
                pltpu.VMEM(((lev_count + 1) * padded, 6 * padded), jnp.bfloat16),
                pltpu.VMEM((2, PAIR, 2 * padded, lats), f32),
                pltpu.VMEM((2, PAIR * 4 * padded, lats), jnp.bfloat16),
                pltpu.VMEM((2, 6 * padded, PAIR * lats), jnp.bfloat16),
                pltpu.VMEM((tiles, own * 2 * lons, LANES), f32),
                pltpu.SemaphoreType.DMA((tiles,)),
            ],
            compiler_params=params(30),
            cost_estimate=spent(20),
            name="mix",
        )(
            jnp.stack(level_starts),
            gradient.reshape(own * 2 * lons, lats),
            balance,
            corr_a,
            corr_b,
            order,
        )
        sent = [mixed[c + len(chunks) :: len(chunks)] for c in range(len(chunks))]

        def send(arrays):
            return [lax.ppermute(array, "lev", along(shift + 1)) for shift, array in enumerate(arrays)]

        final = len(chunks) - 1
        received = [send(arrays) if c < final or final < 2 else None for c, arrays in enumerate(sent)]

    with jax.named_scope("raw"):
        kept = pl.pallas_call(
            functools.partial(raw_kernel, shape, offsets),
            grid=(half // PAIR,),
            out_shape=kept_shapes,
            in_specs=[pl.BlockSpec(memory_space=pltpu.SMEM)]
            + [pl.BlockSpec((own * half, LANES), lambda i, j=j: (0, j)) for j in range(tiles)] * (lev_count - 1)
            + [whole(levels, levels)] * 3
            + [whole(lats, lats)]
            + [pl.BlockSpec((1, PAIR, 2, size, lats), lambda i: (0, i, 0, 0, 0)) for _, size in offsets],
            out_specs=[pl.BlockSpec((1, PAIR, 2, size, lats), lambda i: (0, i, 0, 0, 0)) for _, size in offsets],
            scratch_shapes=[
                pltpu.VMEM((lev_count - 1, 2 * padded, 3 * padded), jnp.bfloat16),
                pltpu.VMEM((PAIR, padded, lats), f32),
                pltpu.VMEM((PAIR * 2 * padded, lats), jnp.bfloat16),
                pltpu.VMEM((3 * padded, PAIR * lats), jnp.bfloat16),
            ],
            input_output_aliases={5 + tiles * (lev_count - 1) + c: c for c in range(len(chunks))},
            compiler_params=params(16),
            cost_estimate=spent(6),
            name="raw",
        )(
            jnp.stack([level_starts[(lev_count - shift) % lev_count] for shift in range(lev_count)]),
            *[part for raw in raws for part in [raw.reshape(own * half, lats)] * tiles],
            balance,
            corr_a,
            corr_b,
            order,
            *mixed[: len(chunks)],
        )

    with jax.named_scope("rates"):
        own_index = lax.dynamic_slice_in_dim(scale_index, me * own, own, 1)
        picks = own_index[:, :, None] == jnp.arange(NSCALE, dtype=jnp.int32)[None, None, :]
        rates = jnp.sum(picks.astype(f32) * scale_table[None, None, :], -1)
        rates = jnp.pad(rates, ((0, 0), (0, padded - own)))
        rates = jnp.broadcast_to(rates[:, :, None], (PASSES, padded, LANES))

    token_shape = jax.ShapeDtypeStruct((ROWS, LANES), f32)
    token_spec = pl.BlockSpec((ROWS, LANES), lambda i: (0, 0))
    result = jnp.zeros((ROWS, LANES), f32)
    token = result

    def sum_specs(parts):
        own_sum = pl.BlockSpec((2, half, 2, ROWS, lats), lambda i: (0, 0, 0, i, 0))
        return [own_sum] + [pl.BlockSpec((3 * half, ROWS, lats), lambda i: (0, i, 0))] * (parts - 1)

    def edges(c, token, passed):
        sums = [kept[c]] + received[c]
        count, start = chunks[c], starts[c]
        halo_shape = jax.ShapeDtypeStruct((halo, 2, count * ROWS, lats), f32)
        fixed = [jax.ShapeDtypeStruct(array.shape, array.dtype) for array in passed]
        with jax.named_scope("edges"):
            first, last, token, *passed = pl.pallas_call(
                functools.partial(edge_kernel, lons, halo, len(sums), len(passed)),
                grid=(count,),
                out_shape=[halo_shape, halo_shape, token_shape, *fixed],
                in_specs=sum_specs(len(sums))
                + [pl.BlockSpec((lons, ROWS, lats), lambda i: (0, start + i, 0))]
                + [hidden] * (3 + len(passed)),
                out_specs=[pl.BlockSpec((halo, 2, ROWS, lats), lambda i: (0, 0, i, 0))] * 2
                + [token_spec]
                + [hidden] * len(passed),
                input_output_aliases={len(sums) + 4 + i: 3 + i for i in range(len(passed))},
                compiler_params=params(12),
                cost_estimate=spent(2),
                name="edges",
            )(*sums, coef, coef_before, coef_after, token, *passed)
            return lax.ppermute(last, "tile", up), lax.ppermute(first, "tile", down), token, passed

    def diffusion(c, before, after, result, token):
        sums = [kept[c]] + received[c]
        count, start = chunks[c], starts[c]
        fixed = lambda i: (0, 0, i, 0)
        level = lambda i: (0, start + i, 0)
        operands = [*sums, coef, before, after, coef_before, coef_after, rates, back, token, result]
        with jax.named_scope("diffusion"):
            return pl.pallas_call(
                functools.partial(diffuse_kernel, lons, lats, len(sums)),
                grid=(count,),
                out_shape=[jax.ShapeDtypeStruct((own * 2 * lons, lats), f32), token_shape],
                in_specs=sum_specs(len(sums))
                + [pl.BlockSpec((lons, ROWS, lats), level)]
                + [pl.BlockSpec((halo, 2, ROWS, lats), fixed)] * 2
                + [pl.BlockSpec((halo - 1, ROWS, lats), level)] * 2
                + [pl.BlockSpec((PASSES, ROWS, LANES), level), whole(lats, lats), hidden, hidden],
                out_specs=[pl.BlockSpec((ROWS * 2 * lons, lats), lambda i: (start + i, 0)), token_spec],
                scratch_shapes=[
                    pltpu.VMEM((lons + 2 * halo, 2, ROWS, lats), f32),
                    pltpu.VMEM((lons + 2 * halo, 2, ROWS, lats), f32),
                    pltpu.VMEM((lons + 2 * halo, ROWS, lats), f32),
                    pltpu.VMEM((tiles * ROWS * 2 * lons, LANES), f32),
                ],
                input_output_aliases={} if c == 0 else {len(operands) - 1: 0},
                compiler_params=params(18),
                cost_estimate=spent(11),
                name="diffusion",
            )(*operands)

    waiting = None
    for c in range(len(chunks)):
        before, after, token, passed = edges(c, token, sent[final] if c == final - 2 else [])
        if c == final - 2:
            received[final] = send(passed)
        if waiting is not None:
            result, token = diffusion(c - 1, *waiting, result, token)
        waiting = (before, after)
    result, _ = diffusion(len(chunks) - 1, *waiting, result, token)
    return result.reshape(own, 2, lons, lats)


def solution(mesh):
    return jax.shard_map(
        on_device,
        mesh=mesh,
        in_specs=(
            P("lev", None, "tile", None),
            P("lev", "tile", None),
            P("lev", "tile", None),
            P(),
            P(),
            P(),
            P(),
            P(),
        ),
        out_specs=P("lev", None, "tile", None),
        check_vma=False,
    )
```

```python
import functools

import jax
import jax.numpy as jnp
import numpy as np
from jax import lax
from jax.experimental import pallas as pl
from jax.experimental.pallas import tpu as pltpu
from jax.sharding import PartitionSpec as P

PASSES = 10
NSCALE = 8
ROWS = 8
LANES = 128
COEF_GROUPS = 4
PAIR = 2
EXACT = lax.Precision.HIGHEST


def chunk_units(total):
    return [2] * (total // 2) + [1] * (total % 2)


def lane_tile(j):
    return slice(j * LANES, (j + 1) * LANES)


def dot_t(a, b):
    return lax.dot_general(
        a, b, (((1,), (1,)), ((), ())), precision=EXACT, preferred_element_type=jnp.float32
    )


def halve(value):
    high = value.astype(jnp.bfloat16)
    return high, (value - high.astype(jnp.float32)).astype(jnp.bfloat16)


def pick_levels(rows, levels, padded, own, starts):
    row = lax.broadcasted_iota(jnp.int32, (rows, levels), 0)
    col = lax.broadcasted_iota(jnp.int32, (rows, levels), 1)
    picked = jnp.zeros((rows, levels), jnp.bool_)
    for s, start in enumerate(starts):
        if start is not None:
            at = row - s * padded
            picked = picked | ((at >= 0) & (at < own) & (col == at + start))
    return picked.astype(jnp.float32)


def three_parts(full, third):
    high, low = halve(full)
    part = lax.broadcasted_iota(jnp.int32, full.shape, 1)
    return jnp.where(part < 2 * third, high.astype(jnp.float32), low.astype(jnp.float32)).astype(jnp.bfloat16)


def dot_exact(a, b):
    return jnp.dot(a, b, precision=EXACT, preferred_element_type=jnp.float32)


def dot_half(a, b):
    return jnp.dot(a, b, preferred_element_type=jnp.float32)


def ordered_parts(lines, plain, order, halves):
    rows, lats = lines.shape[1:]
    for side in range(PAIR):
        high, low = halve(lines[side])
        plain[2 * side * rows : (2 * side + 1) * rows, :] = high
        plain[(2 * side + 1) * rows : (2 * side + 2) * rows, :] = low
    ordered = dot_half(plain[...], order[...])
    for side in range(PAIR):
        place = slice(side * lats, (side + 1) * lats)
        both = ordered[2 * side * rows : 2 * (side + 1) * rows].astype(jnp.bfloat16)
        halves[0 : 2 * rows, place] = both
        halves[2 * rows : 3 * rows, place] = both[0:rows]


def plane(lons, lon, var):
    side, at = divmod(lon, lons // 2)
    group, place = divmod(at, PAIR)
    if side == 0:
        return 3 * PAIR * group + place if var == 0 else None
    return 3 * PAIR * group + PAIR + 2 * place + var


def mix_kernel(shape, offsets, at, *refs):
    levels, own, padded, lons, tiles, targets = shape
    (gradient, bal, cor_a, cor_b, order), refs = refs[:5], refs[5:]
    outs, (weight, weight_raw, lines, plain, halves, grads, sems) = refs[:-7], refs[-7:]
    lats = tiles * LANES
    step = pl.program_id(0)

    @pl.when(step == 0)
    def _():
        arriving = [
            pltpu.make_async_copy(gradient.at[:, lane_tile(j)], grads.at[j], sems.at[j]) for j in range(tiles)
        ]
        for copy in arriving:
            copy.start()
        first = [at[0], None] * 3
        second = [None, at[0]] * 3
        take_first = pick_levels(6 * padded, levels, padded, own, first)
        take_second = pick_levels(6 * padded, levels, padded, own, second)
        pick = pick_levels(targets * padded, levels, padded, own, [at[t] for t in range(targets)])
        cols_a = dot_t(pick, cor_a[...])
        through_a = dot_t(cols_a, take_first + dot_exact(take_second, bal[...]))
        through_b = dot_t(dot_t(pick, cor_b[...]), take_second)
        only_first = dot_t(cols_a, take_first)
        weight[...] = three_parts(jnp.concatenate([through_a, through_b], 0), 2 * padded)
        weight_raw[...] = three_parts(
            jnp.concatenate([through_a[:padded], only_first[padded:], through_b[:padded]], 0), 2 * padded
        )
        lines[...] = jnp.zeros_like(lines)
        for copy in arriving:
            copy.wait()

    for half in range(2):
        for side in range(PAIR):
            lon = half * (lons // 2) + step * PAIR + side
            for var in range(2):
                for j in range(tiles):
                    lines[half, side, pl.ds(var * padded, own), lane_tile(j)] = grads[
                        j, pl.ds(var * lons + lon, own, stride=2 * lons), :
                    ]
        ordered_parts(lines.at[half], plain.at[half], order, halves.at[half])
    for half in range(2):
        mixed = dot_half((weight_raw if half == 0 else weight)[...], halves[half])
        for side in range(PAIR):
            place = slice(side * lats, (side + 1) * lats)
            for target in range(targets):
                for var in range(2):
                    if half == 0 and target > 0 and var == 1:
                        continue
                    first = (var * targets + target) * padded
                    for c, (start, size) in enumerate(offsets):
                        out = outs[target * len(offsets) + c]
                        value = mixed[first + start : first + start + size, place]
                        if target == 0:
                            out[half, side, var] = value
                        else:
                            out[plane(lons, half * (lons // 2) + side, var)] = value


def raw_kernel(shape, offsets, at, *refs):
    levels, own, padded, lons, tiles, targets = shape
    chunks = len(offsets)
    raws, refs = refs[: tiles * (targets - 1)], refs[tiles * (targets - 1) :]
    (bal, cor_a, cor_b, order), kept, outs = refs[:4], refs[4 : 4 + chunks], refs[4 + chunks : 4 + 2 * chunks]
    weight, lines, plain, halves = refs[4 + 2 * chunks :]
    lats = tiles * LANES
    step = pl.program_id(0)

    @pl.when(step == 0)
    def _():
        pick = pick_levels(padded, levels, padded, own, [at[0]])
        cols_a = dot_t(pick, cor_a[...])
        cols_b = dot_t(pick, cor_b[...])
        for source in range(1, targets):
            take = pick_levels(3 * padded, levels, padded, own, [at[source]] * 3)
            full = jnp.concatenate([dot_t(cols_a, dot_exact(take, bal[...])), dot_t(cols_b, take)], 0)
            weight[source - 1] = three_parts(full, padded)
        lines[...] = jnp.zeros_like(lines)

    total = None
    for source in range(targets - 1):
        for side in range(PAIR):
            for j in range(tiles):
                lines[side, 0:own, lane_tile(j)] = raws[source * tiles + j][
                    pl.ds(step * PAIR + side, own, stride=lons // 2), :
                ]
        ordered_parts(lines, plain, order, halves)
        mixed = dot_half(weight[source], halves[...])
        total = mixed if total is None else total + mixed
    for side in range(PAIR):
        place = slice(side * lats, (side + 1) * lats)
        for var in range(2):
            for (start, size), more, out in zip(offsets, kept, outs):
                first = var * padded + start
                out[0, side, var] = more[0, side, var] + total[first : first + size, place]


def even_tile():
    return lax.axis_index("tile") % 2 == 0


def coef_kernel(own, padded, lons, halo, tiles, sea, rough, order, _, coef, near, far, *scratch):
    seas, roughs, lines, values, sems = scratch
    even = even_tile()
    odd = jnp.logical_not(even)
    arriving = []
    for j in range(tiles):
        for source, held in ((sea, seas), (rough, roughs)):
            arriving.append(pltpu.make_async_copy(source.at[:, lane_tile(j)], held.at[j], sems.at[len(arriving)]))
    for copy in arriving:
        copy.start()
    lines[...] = jnp.zeros_like(lines)
    for copy in arriving:
        copy.wait()
    size = lons // COEF_GROUPS
    leaving = []

    def leave(source, *targets):
        sem = sems.at[len(arriving) + len(leaving)]
        copies = [pltpu.make_async_copy(source, target, sem) for target in targets]
        leaving.append(copies)
        act(copies, "start")

    def act(copies, what):
        if len(copies) == 1:
            getattr(copies[0], what)()
        else:
            pl.when(even)(getattr(copies[0], what))
            pl.when(odd)(getattr(copies[1], what))

    for group in range(COEF_GROUPS):
        for at in range(size):
            rows = pl.ds(group * size + at, own, stride=lons)
            for j in range(tiles):
                lines[at * padded : at * padded + own, lane_tile(j)] = (
                    seas[j, rows, :].astype(jnp.float32) * roughs[j, rows, :]
                )
        high, low = halve(lines[...])
        value = dot_half(high, order[...]) + dot_half(low, order[...])
        for at in range(size):
            values[group * size + at] = value[at * padded : (at + 1) * padded]
        start, stop = group * size, (group + 1) * size
        leave(values.at[start:stop], coef.at[start:stop])
        if start < halo:
            until = min(stop, halo)
            leave(values.at[start:until], far.at[start:until], near.at[start:until])
        if stop > lons - halo:
            since = max(start, lons - halo)
            place = slice(since - (lons - halo), stop - (lons - halo))
            leave(values.at[since:stop], near.at[place], far.at[place])
    for copies in leaving:
        act(copies, "wait")


def mixed_at(lons, sums, lon, var):
    value = sums[0][lon // (lons // 2), lon % (lons // 2), var]
    at = plane(lons, lon, var)
    if at is not None:
        for more in sums[1:]:
            value = value + more[at]
    return value


def edge_kernel(lons, halo, parts, passed, *refs):
    sums, coef, (near, far, token) = refs[:parts], refs[parts], refs[parts + 4 + passed : parts + 7 + passed]
    token[...] = jnp.zeros_like(token)

    def give(first, last):
        for lon in range(lons):
            for var in range(2):
                value = coef[lon] * mixed_at(lons, sums, lon, var)
                if lon < halo:
                    first[lon, var] = value
                if lon >= lons - halo:
                    last[lon - (lons - halo), var] = value

    even = even_tile()
    pl.when(even)(lambda: give(far, near))
    pl.when(jnp.logical_not(even))(lambda: give(near, far))


def neighbours(tiles, lane):
    count = len(tiles)
    before = jnp.where(lane == 0, tiles[0], pltpu.roll(tiles[-1], 1, 1))
    after = jnp.where(lane == LANES - 1, tiles[-1], pltpu.roll(tiles[0], LANES - 1, 1))
    line = [before, *tiles, after]
    return [line[j] + line[j + 2] for j in range(count)]


def diffuse(lons, lats, sums, coef, near, far, coef_near, coef_far, rates, weighted, square):
    halo = PASSES
    tiles = lats // LANES
    lane = lax.broadcasted_iota(jnp.int32, (ROWS, LANES), 1)

    for lon in range(lons):
        scale = coef[lon]
        square[halo + lon] = scale * scale
        for var in range(2):
            weighted[0][halo + lon, var] = scale * mixed_at(lons, sums, lon, var)

    def sides(before, after, coef_before, coef_after):
        for lon in range(halo):
            weighted[0][lon] = before[lon]
            weighted[0][halo + lons + lon] = after[lon]
        for lon in range(halo - 1):
            square[1 + lon] = coef_before[lon] * coef_before[lon]
            square[halo + lons + lon] = coef_after[lon] * coef_after[lon]

    even = even_tile()
    pl.when(even)(lambda: sides(far, near, coef_far, coef_near))
    pl.when(jnp.logical_not(even))(lambda: sides(near, far, coef_near, coef_far))

    for section in range(PASSES):
        source, target = weighted[section % 2], weighted[(section + 1) % 2]
        rate = rates[section]
        start = section + 1
        stop = lons + 2 * halo - 1 - section

        def one_variable(var, carry):
            def load(lon):
                return [source[lon, var, :, lane_tile(j)] for j in range(tiles)]

            behind, here = load(start - 1), load(start)
            for lon in range(start, stop):
                ahead = load(lon + 1)
                lat = neighbours(here, lane)
                for j in range(tiles):
                    factor = rate * square[lon, :, lane_tile(j)]
                    spread = (behind[j] + ahead[j]) + lat[j] - 4.0 * here[j]
                    target[lon, var, :, lane_tile(j)] = here[j] + factor * spread
                behind, here = here, ahead
            return carry

        lax.fori_loop(0, 2, one_variable, 0)


def diffuse_kernel(lons, lats, parts, *refs):
    sums, rest = refs[:parts], refs[parts:]
    coef, near, far, coef_near, coef_far, rates, back, _, _, out, token, *rest = rest
    *weighted, square, lines = rest
    tiles = lats // LANES
    token[...] = jnp.zeros_like(token)
    diffuse(lons, lats, sums, coef, near, far, coef_near, coef_far, rates, weighted, square)

    count = ROWS * 2 * lons
    for lon in range(lons):
        scale = coef[lon]
        land = scale == 0.0
        inverse = 1.0 / jnp.where(land, 1.0, scale)
        for var in range(2):
            plain = mixed_at(lons, sums, lon, var)
            value = jnp.where(land, plain, weighted[PASSES % 2][PASSES + lon, var] * inverse)
            for j in range(tiles):
                lines[pl.ds(j * count + var * lons + lon, ROWS, stride=2 * lons), :] = value[:, lane_tile(j)]
    high, low = halve(jnp.concatenate([lines[j * count : (j + 1) * count, :] for j in range(tiles)], 1))
    out[...] = jnp.dot(high, back[...], preferred_element_type=jnp.float32) + jnp.dot(
        low, back[...], preferred_element_type=jnp.float32
    )


def whole(*block):
    return pl.BlockSpec(block, lambda i: (0,) * len(block))


def params(mebibytes):
    return pltpu.CompilerParams(vmem_limit_bytes=mebibytes * 1024 * 1024)


def spent(microseconds):
    return pl.CostEstimate(flops=int(microseconds * 1.153e9), bytes_accessed=1024, transcendentals=0)


def on_device(gradient, land_sea, roughness, scale_index, scale_table, balance, corr_a, corr_b):
    own, _, lons, lats = gradient.shape
    levels = balance.shape[0]
    lev_count = lax.axis_size("lev")
    tile_count = lax.axis_size("tile")
    me = lax.axis_index("lev")
    units = -(-own // ROWS)
    padded = units * ROWS
    chunks = chunk_units(units)
    starts = [sum(chunks[:c]) for c in range(len(chunks))]
    offsets = [(s * ROWS, c * ROWS) for s, c in zip(starts, chunks)]
    halo = PASSES
    unit_bytes = lons * 2 * ROWS * lats * 4
    f32 = jnp.float32
    hidden = pl.BlockSpec(memory_space=pl.ANY)

    def along(shift):
        return [(i, (i + shift) % lev_count) for i in range(lev_count)]

    with jax.named_scope("raw"):
        rows = gradient[:, 1, : lons // 2]
        raws = [lax.ppermute(rows, "lev", along(shift)) for shift in range(1, lev_count)]

    tiles = lats // LANES
    place = np.arange(lats)
    order = np.zeros((lats, lats), np.float32)
    order[place, (place % tiles) * LANES + place // tiles] = 1.0
    back = jnp.asarray(order.T, jnp.bfloat16)
    order = jnp.asarray(order, jnp.bfloat16)

    def swaps(first):
        pairs = [(i, (i + 1) % tile_count) for i in range(first, tile_count, 2)]
        return pairs + [(j, i) for i, j in pairs]

    def exchange(near, far):
        return lax.ppermute(near, "tile", swaps(0)), lax.ppermute(far, "tile", swaps(1))

    with jax.named_scope("coef"):
        coef, near, far = pl.pallas_call(
            functools.partial(coef_kernel, own, padded, lons, halo - 1, tiles),
            out_shape=[
                jax.ShapeDtypeStruct((lons, padded, lats), f32),
                jax.ShapeDtypeStruct((halo - 1, padded, lats), f32),
                jax.ShapeDtypeStruct((halo - 1, padded, lats), f32),
            ],
            in_specs=[hidden, hidden, pl.BlockSpec(memory_space=pltpu.VMEM), hidden],
            out_specs=[hidden] * 3,
            scratch_shapes=[
                pltpu.VMEM((tiles, own * lons, LANES), jnp.int32),
                pltpu.VMEM((tiles, own * lons, LANES), f32),
                pltpu.VMEM((lons // COEF_GROUPS * padded, lats), f32),
                pltpu.VMEM((lons, padded, lats), f32),
                pltpu.SemaphoreType.DMA((2 * tiles + 3 * COEF_GROUPS,)),
            ],
            compiler_params=params(53),
            cost_estimate=spent(10),
            name="coef",
        )(land_sea.reshape(own * lons, lats), roughness.reshape(own * lons, lats), order, rows)
        coef_near, coef_far = exchange(near, far)

    half = lons // 2
    shape = (levels, own, padded, lons, tiles, lev_count)
    kept_shapes = [jax.ShapeDtypeStruct((2, half, 2, size, lats), f32) for _, size in offsets]
    sent_shapes = [jax.ShapeDtypeStruct((3 * half, size, lats), f32) for _, size in offsets]
    kept_specs = [pl.BlockSpec((2, PAIR, 2, size, lats), lambda i: (0, i, 0, 0, 0)) for _, size in offsets]
    sent_specs = [pl.BlockSpec((3 * PAIR, size, lats), lambda i: (i, 0, 0)) for _, size in offsets]
    level_starts = [lax.rem(me + shift, lev_count) * own for shift in range(lev_count)]
    with jax.named_scope("mix"):
        mixed = pl.pallas_call(
            functools.partial(mix_kernel, shape, offsets),
            grid=(half // PAIR,),
            out_shape=kept_shapes + sent_shapes * (lev_count - 1),
            in_specs=[pl.BlockSpec(memory_space=pltpu.SMEM)]
            + [hidden]
            + [whole(levels, levels)] * 3
            + [whole(lats, lats)],
            out_specs=kept_specs + sent_specs * (lev_count - 1),
            scratch_shapes=[
                pltpu.VMEM((2 * lev_count * padded, 6 * padded), jnp.bfloat16),
                pltpu.VMEM(((lev_count + 1) * padded, 6 * padded), jnp.bfloat16),
                pltpu.VMEM((2, PAIR, 2 * padded, lats), f32),
                pltpu.VMEM((2, PAIR * 4 * padded, lats), jnp.bfloat16),
                pltpu.VMEM((2, 6 * padded, PAIR * lats), jnp.bfloat16),
                pltpu.VMEM((tiles, own * 2 * lons, LANES), f32),
                pltpu.SemaphoreType.DMA((tiles,)),
            ],
            compiler_params=params(30),
            cost_estimate=spent(20),
            name="mix",
        )(
            jnp.stack(level_starts),
            gradient.reshape(own * 2 * lons, lats),
            balance,
            corr_a,
            corr_b,
            order,
        )
        sent = [mixed[c + len(chunks) :: len(chunks)] for c in range(len(chunks))]

        def send(arrays):
            return [lax.ppermute(array, "lev", along(shift + 1)) for shift, array in enumerate(arrays)]

        final = len(chunks) - 1
        received = [send(arrays) if c < final or final < 2 else None for c, arrays in enumerate(sent)]

    with jax.named_scope("raw"):
        kept = pl.pallas_call(
            functools.partial(raw_kernel, shape, offsets),
            grid=(half // PAIR,),
            out_shape=kept_shapes,
            in_specs=[pl.BlockSpec(memory_space=pltpu.SMEM)]
            + [pl.BlockSpec((own * half, LANES), lambda i, j=j: (0, j)) for j in range(tiles)] * (lev_count - 1)
            + [whole(levels, levels)] * 3
            + [whole(lats, lats)]
            + [pl.BlockSpec((1, PAIR, 2, size, lats), lambda i: (0, i, 0, 0, 0)) for _, size in offsets],
            out_specs=[pl.BlockSpec((1, PAIR, 2, size, lats), lambda i: (0, i, 0, 0, 0)) for _, size in offsets],
            scratch_shapes=[
                pltpu.VMEM((lev_count - 1, 2 * padded, 3 * padded), jnp.bfloat16),
                pltpu.VMEM((PAIR, padded, lats), f32),
                pltpu.VMEM((PAIR * 2 * padded, lats), jnp.bfloat16),
                pltpu.VMEM((3 * padded, PAIR * lats), jnp.bfloat16),
            ],
            input_output_aliases={5 + tiles * (lev_count - 1) + c: c for c in range(len(chunks))},
            compiler_params=params(16),
            cost_estimate=spent(6),
            name="raw",
        )(
            jnp.stack([level_starts[(lev_count - shift) % lev_count] for shift in range(lev_count)]),
            *[part for raw in raws for part in [raw.reshape(own * half, lats)] * tiles],
            balance,
            corr_a,
            corr_b,
            order,
            *mixed[: len(chunks)],
        )

    with jax.named_scope("rates"):
        own_index = lax.dynamic_slice_in_dim(scale_index, me * own, own, 1)
        picks = own_index[:, :, None] == jnp.arange(NSCALE, dtype=jnp.int32)[None, None, :]
        rates = jnp.sum(picks.astype(f32) * scale_table[None, None, :], -1)
        rates = jnp.pad(rates, ((0, 0), (0, padded - own)))
        rates = jnp.broadcast_to(rates[:, :, None], (PASSES, padded, LANES))

    token_shape = jax.ShapeDtypeStruct((ROWS, LANES), f32)
    token_spec = pl.BlockSpec((ROWS, LANES), lambda i: (0, 0))
    result = jnp.zeros((ROWS, LANES), f32)
    token = result

    def sum_specs(parts):
        own_sum = pl.BlockSpec((2, half, 2, ROWS, lats), lambda i: (0, 0, 0, i, 0))
        return [own_sum] + [pl.BlockSpec((3 * half, ROWS, lats), lambda i: (0, i, 0))] * (parts - 1)

    def edges(c, token, passed):
        sums = [kept[c]] + received[c]
        count, start = chunks[c], starts[c]
        halo_shape = jax.ShapeDtypeStruct((halo, 2, count * ROWS, lats), f32)
        fixed = [jax.ShapeDtypeStruct(array.shape, array.dtype) for array in passed]
        with jax.named_scope("edges"):
            near, far, token, *passed = pl.pallas_call(
                functools.partial(edge_kernel, lons, halo, len(sums), len(passed)),
                grid=(count,),
                out_shape=[halo_shape, halo_shape, token_shape, *fixed],
                in_specs=sum_specs(len(sums))
                + [pl.BlockSpec((lons, ROWS, lats), lambda i: (0, start + i, 0))]
                + [hidden] * (3 + len(passed)),
                out_specs=[pl.BlockSpec((halo, 2, ROWS, lats), lambda i: (0, 0, i, 0))] * 2
                + [token_spec]
                + [hidden] * len(passed),
                input_output_aliases={len(sums) + 4 + i: 3 + i for i in range(len(passed))},
                compiler_params=params(12),
                cost_estimate=spent(2),
                name="edges",
            )(*sums, coef, coef_near, coef_far, token, *passed)
            return *exchange(near, far), token, passed

    def diffusion(c, near, far, result, token):
        sums = [kept[c]] + received[c]
        count, start = chunks[c], starts[c]
        level = lambda i: (0, start + i, 0)
        operands = [*sums, coef, near, far, coef_near, coef_far, rates, back, token, result]
        with jax.named_scope("diffusion"):
            return pl.pallas_call(
                functools.partial(diffuse_kernel, lons, lats, len(sums)),
                grid=(count,),
                out_shape=[jax.ShapeDtypeStruct((own * 2 * lons, lats), f32), token_shape],
                in_specs=sum_specs(len(sums))
                + [pl.BlockSpec((lons, ROWS, lats), level)]
                + [pl.BlockSpec((halo, 2, ROWS, lats), lambda i: (0, 0, i, 0))] * 2
                + [pl.BlockSpec((halo - 1, ROWS, lats), level)] * 2
                + [pl.BlockSpec((PASSES, ROWS, LANES), level), whole(lats, lats), hidden, hidden],
                out_specs=[pl.BlockSpec((ROWS * 2 * lons, lats), lambda i: (start + i, 0)), token_spec],
                scratch_shapes=[
                    pltpu.VMEM((lons + 2 * halo, 2, ROWS, lats), f32),
                    pltpu.VMEM((lons + 2 * halo, 2, ROWS, lats), f32),
                    pltpu.VMEM((lons + 2 * halo, ROWS, lats), f32),
                    pltpu.VMEM((tiles * ROWS * 2 * lons, LANES), f32),
                ],
                input_output_aliases={} if c == 0 else {len(operands) - 1: 0},
                compiler_params=params(18),
                cost_estimate=spent(11),
                name="diffusion",
            )(*operands)

    waiting = None
    for c in range(len(chunks)):
        near, far, token, passed = edges(c, token, sent[final] if c == final - 2 else [])
        if c == final - 2:
            received[final] = send(passed)
        if waiting is not None:
            result, token = diffusion(c - 1, *waiting, result, token)
        waiting = (near, far)
    result, _ = diffusion(len(chunks) - 1, *waiting, result, token)
    return result.reshape(own, 2, lons, lats)


def solution(mesh):
    return jax.shard_map(
        on_device,
        mesh=mesh,
        in_specs=(
            P("lev", None, "tile", None),
            P("lev", "tile", None),
            P("lev", "tile", None),
            P(),
            P(),
            P(),
            P(),
            P(),
        ),
        out_specs=P("lev", None, "tile", None),
        check_vma=False,
    )
```

```python
import functools

import jax
import jax.numpy as jnp
import numpy as np
from jax import lax
from jax.experimental import pallas as pl
from jax.experimental.pallas import tpu as pltpu
from jax.sharding import PartitionSpec as P

PASSES = 10
NSCALE = 8
ROWS = 8
LANES = 128
COEF_GROUPS = 4
PAIR = 2
EXACT = lax.Precision.HIGHEST


def chunk_units(total):
    return [2] * (total // 2) + [1] * (total % 2)


def lane_tile(j):
    return slice(j * LANES, (j + 1) * LANES)


def dot_t(a, b):
    return lax.dot_general(
        a, b, (((1,), (1,)), ((), ())), precision=EXACT, preferred_element_type=jnp.float32
    )


def halve(value):
    high = value.astype(jnp.bfloat16)
    return high, (value - high.astype(jnp.float32)).astype(jnp.bfloat16)


def pick_levels(rows, levels, padded, own, starts):
    row = lax.broadcasted_iota(jnp.int32, (rows, levels), 0)
    col = lax.broadcasted_iota(jnp.int32, (rows, levels), 1)
    picked = jnp.zeros((rows, levels), jnp.bool_)
    for s, start in enumerate(starts):
        if start is not None:
            at = row - s * padded
            picked = picked | ((at >= 0) & (at < own) & (col == at + start))
    return picked.astype(jnp.float32)


def three_parts(full, third):
    high, low = halve(full)
    part = lax.broadcasted_iota(jnp.int32, full.shape, 1)
    return jnp.where(part < 2 * third, high.astype(jnp.float32), low.astype(jnp.float32)).astype(jnp.bfloat16)


def dot_exact(a, b):
    return jnp.dot(a, b, precision=EXACT, preferred_element_type=jnp.float32)


def dot_half(a, b):
    return jnp.dot(a, b, preferred_element_type=jnp.float32)


def ordered_parts(lines, plain, order, halves):
    rows, lats = lines.shape[1:]
    for side in range(PAIR):
        high, low = halve(lines[side])
        plain[2 * side * rows : (2 * side + 1) * rows, :] = high
        plain[(2 * side + 1) * rows : (2 * side + 2) * rows, :] = low
    ordered = dot_half(plain[...], order[...])
    for side in range(PAIR):
        place = slice(side * lats, (side + 1) * lats)
        both = ordered[2 * side * rows : 2 * (side + 1) * rows].astype(jnp.bfloat16)
        halves[0 : 2 * rows, place] = both
        halves[2 * rows : 3 * rows, place] = both[0:rows]


def plane(lons, lon, var):
    side, at = divmod(lon, lons // 2)
    group, place = divmod(at, PAIR)
    if side == 0:
        return 3 * PAIR * group + place if var == 0 else None
    return 3 * PAIR * group + PAIR + 2 * place + var


def mix_kernel(shape, offsets, at, *refs):
    levels, own, padded, lons, tiles, targets = shape
    (gradient, bal, cor_a, cor_b, order), refs = refs[:5], refs[5:]
    outs, (weight, weight_raw, lines, plain, halves, grads, sems) = refs[:-7], refs[-7:]
    lats = tiles * LANES
    step = pl.program_id(0)

    @pl.when(step == 0)
    def _():
        arriving = [
            pltpu.make_async_copy(gradient.at[:, lane_tile(j)], grads.at[j], sems.at[j]) for j in range(tiles)
        ]
        for copy in arriving:
            copy.start()
        first = [at[0], None] * 3
        second = [None, at[0]] * 3
        take_first = pick_levels(6 * padded, levels, padded, own, first)
        take_second = pick_levels(6 * padded, levels, padded, own, second)
        pick = pick_levels(targets * padded, levels, padded, own, [at[t] for t in range(targets)])
        cols_a = dot_t(pick, cor_a[...])
        through_a = dot_t(cols_a, take_first + dot_exact(take_second, bal[...]))
        through_b = dot_t(dot_t(pick, cor_b[...]), take_second)
        only_first = dot_t(cols_a, take_first)
        weight[...] = three_parts(jnp.concatenate([through_a, through_b], 0), 2 * padded)
        weight_raw[...] = three_parts(
            jnp.concatenate([through_a[:padded], only_first[padded:], through_b[:padded]], 0), 2 * padded
        )
        lines[...] = jnp.zeros_like(lines)
        for copy in arriving:
            copy.wait()

    for half in range(2):
        for side in range(PAIR):
            lon = half * (lons // 2) + step * PAIR + side
            for var in range(2):
                for j in range(tiles):
                    lines[half, side, pl.ds(var * padded, own), lane_tile(j)] = grads[
                        j, pl.ds(var * lons + lon, own, stride=2 * lons), :
                    ]
        ordered_parts(lines.at[half], plain.at[half], order, halves.at[half])
    for half in range(2):
        mixed = dot_half((weight_raw if half == 0 else weight)[...], halves[half])
        for side in range(PAIR):
            place = slice(side * lats, (side + 1) * lats)
            for target in range(targets):
                for var in range(2):
                    if half == 0 and target > 0 and var == 1:
                        continue
                    first = (var * targets + target) * padded
                    for c, (start, size) in enumerate(offsets):
                        out = outs[target * len(offsets) + c]
                        value = mixed[first + start : first + start + size, place]
                        if target == 0:
                            out[half, side, var] = value
                        else:
                            out[plane(lons, half * (lons // 2) + side, var)] = value


def raw_kernel(shape, offsets, at, *refs):
    levels, own, padded, lons, tiles, targets = shape
    chunks = len(offsets)
    raws, refs = refs[: tiles * (targets - 1)], refs[tiles * (targets - 1) :]
    (bal, cor_a, cor_b, order), kept, outs = refs[:4], refs[4 : 4 + chunks], refs[4 + chunks : 4 + 2 * chunks]
    weight, lines, plain, halves = refs[4 + 2 * chunks :]
    lats = tiles * LANES
    step = pl.program_id(0)

    @pl.when(step == 0)
    def _():
        pick = pick_levels(padded, levels, padded, own, [at[0]])
        cols_a = dot_t(pick, cor_a[...])
        cols_b = dot_t(pick, cor_b[...])
        for source in range(1, targets):
            take = pick_levels(3 * padded, levels, padded, own, [at[source]] * 3)
            full = jnp.concatenate([dot_t(cols_a, dot_exact(take, bal[...])), dot_t(cols_b, take)], 0)
            weight[source - 1] = three_parts(full, padded)
        lines[...] = jnp.zeros_like(lines)

    total = None
    for source in range(targets - 1):
        for side in range(PAIR):
            for j in range(tiles):
                lines[side, 0:own, lane_tile(j)] = raws[source * tiles + j][
                    pl.ds(step * PAIR + side, own, stride=lons // 2), :
                ]
        ordered_parts(lines, plain, order, halves)
        mixed = dot_half(weight[source], halves[...])
        total = mixed if total is None else total + mixed
    for side in range(PAIR):
        place = slice(side * lats, (side + 1) * lats)
        for var in range(2):
            for (start, size), more, out in zip(offsets, kept, outs):
                first = var * padded + start
                out[0, side, var] = more[0, side, var] + total[first : first + size, place]


def coef_kernel(own, padded, lons, halo, tiles, sea, rough, order, _, coef, first, last, seas, roughs, lines, values, sems):
    arriving = []
    for j in range(tiles):
        for source, held in ((sea, seas), (rough, roughs)):
            arriving.append(pltpu.make_async_copy(source.at[:, lane_tile(j)], held.at[j], sems.at[len(arriving)]))
    for copy in arriving:
        copy.start()
    lines[...] = jnp.zeros_like(lines)
    for copy in arriving:
        copy.wait()
    size = lons // COEF_GROUPS
    leaving = []

    def leave(source, target):
        copy = pltpu.make_async_copy(source, target, sems.at[len(arriving) + len(leaving)])
        copy.start()
        leaving.append(copy)

    for group in range(COEF_GROUPS):
        for at in range(size):
            rows = pl.ds(group * size + at, own, stride=lons)
            for j in range(tiles):
                lines[at * padded : at * padded + own, lane_tile(j)] = (
                    seas[j, rows, :].astype(jnp.float32) * roughs[j, rows, :]
                )
        high, low = halve(lines[...])
        value = dot_half(high, order[...]) + dot_half(low, order[...])
        for at in range(size):
            values[group * size + at] = value[at * padded : (at + 1) * padded]
        start, stop = group * size, (group + 1) * size
        leave(values.at[start:stop], coef.at[start:stop])
        if start < halo:
            until = min(stop, halo)
            leave(values.at[start:until], first.at[start:until])
        if stop > lons - halo:
            since = max(start, lons - halo)
            leave(values.at[since:stop], last.at[since - (lons - halo) : stop - (lons - halo)])
    for copy in leaving:
        copy.wait()


def mixed_at(lons, sums, lon, var):
    value = sums[0][lon // (lons // 2), lon % (lons // 2), var]
    at = plane(lons, lon, var)
    if at is not None:
        for more in sums[1:]:
            value = value + more[at]
    return value


def edge_kernel(lons, halo, parts, passed, *refs):
    sums, coef, (first, last, token) = refs[:parts], refs[parts], refs[parts + 4 + passed : parts + 7 + passed]
    token[...] = jnp.zeros_like(token)
    for lon in range(lons):
        for var in range(2):
            value = coef[lon] * mixed_at(lons, sums, lon, var)
            if lon < halo:
                first[lon, var] = value
            if lon >= lons - halo:
                last[lon - (lons - halo), var] = value


def neighbours(tiles, lane):
    count = len(tiles)
    before = jnp.where(lane == 0, tiles[0], pltpu.roll(tiles[-1], 1, 1))
    after = jnp.where(lane == LANES - 1, tiles[-1], pltpu.roll(tiles[0], LANES - 1, 1))
    line = [before, *tiles, after]
    return [line[j] + line[j + 2] for j in range(count)]


def diffuse(lons, lats, sums, coef, before, after, coef_before, coef_after, rates, weighted, square):
    halo = PASSES
    tiles = lats // LANES
    lane = lax.broadcasted_iota(jnp.int32, (ROWS, LANES), 1)

    for lon in range(lons):
        scale = coef[lon]
        square[halo + lon] = scale * scale
        for var in range(2):
            weighted[0][halo + lon, var] = scale * mixed_at(lons, sums, lon, var)
    for lon in range(halo):
        weighted[0][lon] = before[lon]
        weighted[0][halo + lons + lon] = after[lon]
    for lon in range(halo - 1):
        square[1 + lon] = coef_before[lon] * coef_before[lon]
        square[halo + lons + lon] = coef_after[lon] * coef_after[lon]

    for section in range(PASSES):
        source, target = weighted[section % 2], weighted[(section + 1) % 2]
        rate = rates[section]
        start = section + 1
        stop = lons + 2 * halo - 1 - section

        def one_variable(var, carry):
            def load(lon):
                return [source[lon, var, :, lane_tile(j)] for j in range(tiles)]

            behind, here = load(start - 1), load(start)
            for lon in range(start, stop):
                ahead = load(lon + 1)
                lat = neighbours(here, lane)
                for j in range(tiles):
                    factor = rate * square[lon, :, lane_tile(j)]
                    spread = (behind[j] + ahead[j]) + lat[j] - 4.0 * here[j]
                    target[lon, var, :, lane_tile(j)] = here[j] + factor * spread
                behind, here = here, ahead
            return carry

        lax.fori_loop(0, 2, one_variable, 0)


def diffuse_kernel(lons, lats, parts, *refs):
    sums, rest = refs[:parts], refs[parts:]
    coef, before, after, coef_before, coef_after, rates, back, _, _, out, token, *rest = rest
    *weighted, square, lines = rest
    tiles = lats // LANES
    token[...] = jnp.zeros_like(token)
    diffuse(lons, lats, sums, coef, before, after, coef_before, coef_after, rates, weighted, square)

    count = ROWS * 2 * lons
    for lon in range(lons):
        scale = coef[lon]
        land = scale == 0.0
        inverse = 1.0 / jnp.where(land, 1.0, scale)
        for var in range(2):
            plain = mixed_at(lons, sums, lon, var)
            value = jnp.where(land, plain, weighted[PASSES % 2][PASSES + lon, var] * inverse)
            for j in range(tiles):
                lines[pl.ds(j * count + var * lons + lon, ROWS, stride=2 * lons), :] = value[:, lane_tile(j)]
    high, low = halve(jnp.concatenate([lines[j * count : (j + 1) * count, :] for j in range(tiles)], 1))
    out[...] = jnp.dot(high, back[...], preferred_element_type=jnp.float32) + jnp.dot(
        low, back[...], preferred_element_type=jnp.float32
    )


def whole(*block):
    return pl.BlockSpec(block, lambda i: (0,) * len(block))


def params(mebibytes):
    return pltpu.CompilerParams(vmem_limit_bytes=mebibytes * 1024 * 1024)


def spent(microseconds):
    return pl.CostEstimate(flops=int(microseconds * 1.153e9), bytes_accessed=1024, transcendentals=0)


def on_device(gradient, land_sea, roughness, scale_index, scale_table, balance, corr_a, corr_b):
    own, _, lons, lats = gradient.shape
    levels = balance.shape[0]
    lev_count = lax.axis_size("lev")
    tile_count = lax.axis_size("tile")
    me = lax.axis_index("lev")
    units = -(-own // ROWS)
    padded = units * ROWS
    chunks = chunk_units(units)
    starts = [sum(chunks[:c]) for c in range(len(chunks))]
    offsets = [(s * ROWS, c * ROWS) for s, c in zip(starts, chunks)]
    halo = PASSES
    unit_bytes = lons * 2 * ROWS * lats * 4
    f32 = jnp.float32
    hidden = pl.BlockSpec(memory_space=pl.ANY)

    def along(shift):
        return [(i, (i + shift) % lev_count) for i in range(lev_count)]

    with jax.named_scope("raw"):
        rows = gradient[:, 1, : lons // 2]
        raws = [lax.ppermute(rows, "lev", along(shift)) for shift in range(1, lev_count)]

    tiles = lats // LANES
    place = np.arange(lats)
    order = np.zeros((lats, lats), np.float32)
    order[place, (place % tiles) * LANES + place // tiles] = 1.0
    back = jnp.asarray(order.T, jnp.bfloat16)
    order = jnp.asarray(order, jnp.bfloat16)

    up = [(i, (i + 1) % tile_count) for i in range(tile_count)]
    down = [(j, i) for i, j in up]
    with jax.named_scope("coef"):
        coef, first, last = pl.pallas_call(
            functools.partial(coef_kernel, own, padded, lons, halo - 1, tiles),
            out_shape=[
                jax.ShapeDtypeStruct((lons, padded, lats), f32),
                jax.ShapeDtypeStruct((halo - 1, padded, lats), f32),
                jax.ShapeDtypeStruct((halo - 1, padded, lats), f32),
            ],
            in_specs=[hidden, hidden, pl.BlockSpec(memory_space=pltpu.VMEM), hidden],
            out_specs=[hidden] * 3,
            scratch_shapes=[
                pltpu.VMEM((tiles, own * lons, LANES), jnp.int32),
                pltpu.VMEM((tiles, own * lons, LANES), f32),
                pltpu.VMEM((lons // COEF_GROUPS * padded, lats), f32),
                pltpu.VMEM((lons, padded, lats), f32),
                pltpu.SemaphoreType.DMA((2 * tiles + 3 * COEF_GROUPS,)),
            ],
            compiler_params=params(20),
            cost_estimate=spent(10),
            name="coef",
        )(land_sea.reshape(own * lons, lats), roughness.reshape(own * lons, lats), order, rows)
        coef_before = lax.ppermute(last, "tile", up)
        coef_after = lax.ppermute(first, "tile", down)

    half = lons // 2
    shape = (levels, own, padded, lons, tiles, lev_count)
    kept_shapes = [jax.ShapeDtypeStruct((2, half, 2, size, lats), f32) for _, size in offsets]
    sent_shapes = [jax.ShapeDtypeStruct((3 * half, size, lats), f32) for _, size in offsets]
    kept_specs = [pl.BlockSpec((2, PAIR, 2, size, lats), lambda i: (0, i, 0, 0, 0)) for _, size in offsets]
    sent_specs = [pl.BlockSpec((3 * PAIR, size, lats), lambda i: (i, 0, 0)) for _, size in offsets]
    level_starts = [lax.rem(me + shift, lev_count) * own for shift in range(lev_count)]
    with jax.named_scope("mix"):
        mixed = pl.pallas_call(
            functools.partial(mix_kernel, shape, offsets),
            grid=(half // PAIR,),
            out_shape=kept_shapes + sent_shapes * (lev_count - 1),
            in_specs=[pl.BlockSpec(memory_space=pltpu.SMEM)]
            + [hidden]
            + [whole(levels, levels)] * 3
            + [whole(lats, lats)],
            out_specs=kept_specs + sent_specs * (lev_count - 1),
            scratch_shapes=[
                pltpu.VMEM((2 * lev_count * padded, 6 * padded), jnp.bfloat16),
                pltpu.VMEM(((lev_count + 1) * padded, 6 * padded), jnp.bfloat16),
                pltpu.VMEM((2, PAIR, 2 * padded, lats), f32),
                pltpu.VMEM((2, PAIR * 4 * padded, lats), jnp.bfloat16),
                pltpu.VMEM((2, 6 * padded, PAIR * lats), jnp.bfloat16),
                pltpu.VMEM((tiles, own * 2 * lons, LANES), f32),
                pltpu.SemaphoreType.DMA((tiles,)),
            ],
            compiler_params=params(30),
            cost_estimate=spent(20),
            name="mix",
        )(
            jnp.stack(level_starts),
            gradient.reshape(own * 2 * lons, lats),
            balance,
            corr_a,
            corr_b,
            order,
        )
        sent = [mixed[c + len(chunks) :: len(chunks)] for c in range(len(chunks))]

        def send(arrays):
            return [lax.ppermute(array, "lev", along(shift + 1)) for shift, array in enumerate(arrays)]

        final = len(chunks) - 1
        received = [send(arrays) if c < final or final < 2 else None for c, arrays in enumerate(sent)]

    with jax.named_scope("raw"):
        kept = pl.pallas_call(
            functools.partial(raw_kernel, shape, offsets),
            grid=(half // PAIR,),
            out_shape=kept_shapes,
            in_specs=[pl.BlockSpec(memory_space=pltpu.SMEM)]
            + [pl.BlockSpec((own * half, LANES), lambda i, j=j: (0, j)) for j in range(tiles)] * (lev_count - 1)
            + [whole(levels, levels)] * 3
            + [whole(lats, lats)]
            + [pl.BlockSpec((1, PAIR, 2, size, lats), lambda i: (0, i, 0, 0, 0)) for _, size in offsets],
            out_specs=[pl.BlockSpec((1, PAIR, 2, size, lats), lambda i: (0, i, 0, 0, 0)) for _, size in offsets],
            scratch_shapes=[
                pltpu.VMEM((lev_count - 1, 2 * padded, 3 * padded), jnp.bfloat16),
                pltpu.VMEM((PAIR, padded, lats), f32),
                pltpu.VMEM((PAIR * 2 * padded, lats), jnp.bfloat16),
                pltpu.VMEM((3 * padded, PAIR * lats), jnp.bfloat16),
            ],
            input_output_aliases={5 + tiles * (lev_count - 1) + c: c for c in range(len(chunks))},
            compiler_params=params(16),
            cost_estimate=spent(6),
            name="raw",
        )(
            jnp.stack([level_starts[(lev_count - shift) % lev_count] for shift in range(lev_count)]),
            *[part for raw in raws for part in [raw.reshape(own * half, lats)] * tiles],
            balance,
            corr_a,
            corr_b,
            order,
            *mixed[: len(chunks)],
        )

    with jax.named_scope("rates"):
        own_index = lax.dynamic_slice_in_dim(scale_index, me * own, own, 1)
        picks = own_index[:, :, None] == jnp.arange(NSCALE, dtype=jnp.int32)[None, None, :]
        rates = jnp.sum(picks.astype(f32) * scale_table[None, None, :], -1)
        rates = jnp.pad(rates, ((0, 0), (0, padded - own)))
        rates = jnp.broadcast_to(rates[:, :, None], (PASSES, padded, LANES))

    token_shape = jax.ShapeDtypeStruct((ROWS, LANES), f32)
    token_spec = pl.BlockSpec((ROWS, LANES), lambda i: (0, 0))
    result = jnp.zeros((ROWS, LANES), f32)
    token = result

    def sum_specs(parts):
        own_sum = pl.BlockSpec((2, half, 2, ROWS, lats), lambda i: (0, 0, 0, i, 0))
        return [own_sum] + [pl.BlockSpec((3 * half, ROWS, lats), lambda i: (0, i, 0))] * (parts - 1)

    def edges(c, token, passed):
        sums = [kept[c]] + received[c]
        count, start = chunks[c], starts[c]
        halo_shape = jax.ShapeDtypeStruct((halo, 2, count * ROWS, lats), f32)
        fixed = [jax.ShapeDtypeStruct(array.shape, array.dtype) for array in passed]
        with jax.named_scope("edges"):
            first, last, token, *passed = pl.pallas_call(
                functools.partial(edge_kernel, lons, halo, len(sums), len(passed)),
                grid=(count,),
                out_shape=[halo_shape, halo_shape, token_shape, *fixed],
                in_specs=sum_specs(len(sums))
                + [pl.BlockSpec((lons, ROWS, lats), lambda i: (0, start + i, 0))]
                + [hidden] * (3 + len(passed)),
                out_specs=[pl.BlockSpec((halo, 2, ROWS, lats), lambda i: (0, 0, i, 0))] * 2
                + [token_spec]
                + [hidden] * len(passed),
                input_output_aliases={len(sums) + 4 + i: 3 + i for i in range(len(passed))},
                compiler_params=params(12),
                cost_estimate=spent(2),
                name="edges",
            )(*sums, coef, coef_before, coef_after, token, *passed)
            return lax.ppermute(last, "tile", up), lax.ppermute(first, "tile", down), token, passed

    def diffusion(c, before, after, result, token):
        sums = [kept[c]] + received[c]
        count, start = chunks[c], starts[c]
        fixed = lambda i: (0, 0, i, 0)
        level = lambda i: (0, start + i, 0)
        operands = [*sums, coef, before, after, coef_before, coef_after, rates, back, token, result]
        with jax.named_scope("diffusion"):
            return pl.pallas_call(
                functools.partial(diffuse_kernel, lons, lats, len(sums)),
                grid=(count,),
                out_shape=[jax.ShapeDtypeStruct((own * 2 * lons, lats), f32), token_shape],
                in_specs=sum_specs(len(sums))
                + [pl.BlockSpec((lons, ROWS, lats), level)]
                + [pl.BlockSpec((halo, 2, ROWS, lats), fixed)] * 2
                + [pl.BlockSpec((halo - 1, ROWS, lats), level)] * 2
                + [pl.BlockSpec((PASSES, ROWS, LANES), level), whole(lats, lats), hidden, hidden],
                out_specs=[pl.BlockSpec((ROWS * 2 * lons, lats), lambda i: (start + i, 0)), token_spec],
                scratch_shapes=[
                    pltpu.VMEM((lons + 2 * halo, 2, ROWS, lats), f32),
                    pltpu.VMEM((lons + 2 * halo, 2, ROWS, lats), f32),
                    pltpu.VMEM((lons + 2 * halo, ROWS, lats), f32),
                    pltpu.VMEM((tiles * ROWS * 2 * lons, LANES), f32),
                ],
                input_output_aliases={} if c == 0 else {len(operands) - 1: 0},
                compiler_params=params(18),
                cost_estimate=spent(11),
                name="diffusion",
            )(*operands)

    waiting = None
    for c in range(len(chunks)):
        before, after, token, passed = edges(c, token, sent[final] if c == final - 2 else [])
        if c == final - 2:
            received[final] = send(passed)
        if waiting is not None:
            result, token = diffusion(c - 1, *waiting, result, token)
        waiting = (before, after)
    result, _ = diffusion(len(chunks) - 1, *waiting, result, token)
    return result.reshape(own, 2, lons, lats)


def solution(mesh):
    return jax.shard_map(
        on_device,
        mesh=mesh,
        in_specs=(
            P("lev", None, "tile", None),
            P("lev", "tile", None),
            P("lev", "tile", None),
            P(),
            P(),
            P(),
            P(),
            P(),
        ),
        out_specs=P("lev", None, "tile", None),
        check_vma=False,
    )
```

```python
import functools

import jax
import jax.numpy as jnp
import numpy as np
from jax import lax
from jax.experimental import pallas as pl
from jax.experimental.pallas import tpu as pltpu
from jax.sharding import PartitionSpec as P

PASSES = 10
NSCALE = 8
ROWS = 8
LANES = 128
COEF_GROUPS = 4
PAIR = 2
EXACT = lax.Precision.HIGHEST


def chunk_units(total):
    return [2] * (total // 2) + [1] * (total % 2)


def lane_tile(j):
    return slice(j * LANES, (j + 1) * LANES)


def dot_t(a, b):
    return lax.dot_general(
        a, b, (((1,), (1,)), ((), ())), precision=EXACT, preferred_element_type=jnp.float32
    )


def halve(value):
    high = value.astype(jnp.bfloat16)
    return high, (value - high.astype(jnp.float32)).astype(jnp.bfloat16)


def pick_levels(rows, levels, padded, own, starts):
    row = lax.broadcasted_iota(jnp.int32, (rows, levels), 0)
    col = lax.broadcasted_iota(jnp.int32, (rows, levels), 1)
    picked = jnp.zeros((rows, levels), jnp.bool_)
    for s, start in enumerate(starts):
        if start is not None:
            at = row - s * padded
            picked = picked | ((at >= 0) & (at < own) & (col == at + start))
    return picked.astype(jnp.float32)


def three_parts(full, third):
    high, low = halve(full)
    part = lax.broadcasted_iota(jnp.int32, full.shape, 1)
    return jnp.where(part < 2 * third, high.astype(jnp.float32), low.astype(jnp.float32)).astype(jnp.bfloat16)


def dot_exact(a, b):
    return jnp.dot(a, b, precision=EXACT, preferred_element_type=jnp.float32)


def dot_half(a, b):
    return jnp.dot(a, b, preferred_element_type=jnp.float32)


def ordered_parts(lines, plain, order, halves):
    rows, lats = lines.shape[1:]
    for side in range(PAIR):
        high, low = halve(lines[side])
        plain[2 * side * rows : (2 * side + 1) * rows, :] = high
        plain[(2 * side + 1) * rows : (2 * side + 2) * rows, :] = low
    ordered = dot_half(plain[...], order[...])
    for side in range(PAIR):
        place = slice(side * lats, (side + 1) * lats)
        both = ordered[2 * side * rows : 2 * (side + 1) * rows].astype(jnp.bfloat16)
        halves[0 : 2 * rows, place] = both
        halves[2 * rows : 3 * rows, place] = both[0:rows]


def plane(lons, lon, var):
    side, at = divmod(lon, lons // 2)
    group, place = divmod(at, PAIR)
    if side == 0:
        return 3 * PAIR * group + place if var == 0 else None
    return 3 * PAIR * group + PAIR + 2 * place + var


def mix_kernel(shape, offsets, at, *refs):
    levels, own, padded, lons, tiles, targets = shape
    (gradient, bal, cor_a, cor_b, order), refs = refs[:5], refs[5:]
    outs, (weight, weight_raw, lines, plain, halves, grads, sems) = refs[:-7], refs[-7:]
    lats = tiles * LANES
    step = pl.program_id(0)

    @pl.when(step == 0)
    def _():
        arriving = [
            pltpu.make_async_copy(gradient.at[:, lane_tile(j)], grads.at[j], sems.at[j]) for j in range(tiles)
        ]
        for copy in arriving:
            copy.start()
        first = [at[0], None] * 3
        second = [None, at[0]] * 3
        take_first = pick_levels(6 * padded, levels, padded, own, first)
        take_second = pick_levels(6 * padded, levels, padded, own, second)
        pick = pick_levels(targets * padded, levels, padded, own, [at[t] for t in range(targets)])
        cols_a = dot_t(pick, cor_a[...])
        through_a = dot_t(cols_a, take_first + dot_exact(take_second, bal[...]))
        through_b = dot_t(dot_t(pick, cor_b[...]), take_second)
        only_first = dot_t(cols_a, take_first)
        weight[...] = three_parts(jnp.concatenate([through_a, through_b], 0), 2 * padded)
        weight_raw[...] = three_parts(
            jnp.concatenate([through_a[:padded], only_first[padded:], through_b[:padded]], 0), 2 * padded
        )
        lines[...] = jnp.zeros_like(lines)
        for copy in arriving:
            copy.wait()

    for half in range(2):
        for side in range(PAIR):
            lon = half * (lons // 2) + step * PAIR + side
            for var in range(2):
                for j in range(tiles):
                    lines[half, side, pl.ds(var * padded, own), lane_tile(j)] = grads[
                        j, pl.ds(var * lons + lon, own, stride=2 * lons), :
                    ]
        ordered_parts(lines.at[half], plain.at[half], order, halves.at[half])
    for half in range(2):
        mixed = dot_half((weight_raw if half == 0 else weight)[...], halves[half])
        for side in range(PAIR):
            place = slice(side * lats, (side + 1) * lats)
            for target in range(targets):
                for var in range(2):
                    if half == 0 and target > 0 and var == 1:
                        continue
                    first = (var * targets + target) * padded
                    for c, (start, size) in enumerate(offsets):
                        out = outs[target * len(offsets) + c]
                        value = mixed[first + start : first + start + size, place]
                        if target == 0:
                            out[half, side, var] = value
                        else:
                            out[plane(lons, half * (lons // 2) + side, var)] = value


def raw_kernel(shape, offsets, at, *refs):
    levels, own, padded, lons, tiles, targets = shape
    chunks = len(offsets)
    raws, refs = refs[: tiles * (targets - 1)], refs[tiles * (targets - 1) :]
    (bal, cor_a, cor_b, order), kept, outs = refs[:4], refs[4 : 4 + chunks], refs[4 + chunks : 4 + 2 * chunks]
    weight, lines, plain, halves = refs[4 + 2 * chunks :]
    lats = tiles * LANES
    step = pl.program_id(0)

    @pl.when(step == 0)
    def _():
        pick = pick_levels(padded, levels, padded, own, [at[0]])
        cols_a = dot_t(pick, cor_a[...])
        cols_b = dot_t(pick, cor_b[...])
        for source in range(1, targets):
            take = pick_levels(3 * padded, levels, padded, own, [at[source]] * 3)
            full = jnp.concatenate([dot_t(cols_a, dot_exact(take, bal[...])), dot_t(cols_b, take)], 0)
            weight[source - 1] = three_parts(full, padded)
        lines[...] = jnp.zeros_like(lines)

    total = None
    for source in range(targets - 1):
        for side in range(PAIR):
            for j in range(tiles):
                lines[side, 0:own, lane_tile(j)] = raws[source * tiles + j][
                    pl.ds(step * PAIR + side, own, stride=lons // 2), :
                ]
        ordered_parts(lines, plain, order, halves)
        mixed = dot_half(weight[source], halves[...])
        total = mixed if total is None else total + mixed
    for side in range(PAIR):
        place = slice(side * lats, (side + 1) * lats)
        for var in range(2):
            for (start, size), more, out in zip(offsets, kept, outs):
                first = var * padded + start
                out[0, side, var] = more[0, side, var] + total[first : first + size, place]


def coef_kernel(own, padded, lons, halo, tiles, sea, rough, order, _, coef, first, last, seas, roughs, lines, values, sems):
    arriving = []
    for j in range(tiles):
        for source, held in ((sea, seas), (rough, roughs)):
            arriving.append(pltpu.make_async_copy(source.at[:, lane_tile(j)], held.at[j], sems.at[len(arriving)]))
    for copy in arriving:
        copy.start()
    lines[...] = jnp.zeros_like(lines)
    for copy in arriving:
        copy.wait()
    size = lons // COEF_GROUPS
    leaving = []

    def leave(source, target):
        copy = pltpu.make_async_copy(source, target, sems.at[len(arriving) + len(leaving)])
        copy.start()
        leaving.append(copy)

    for group in range(COEF_GROUPS):
        for at in range(size):
            rows = pl.ds(group * size + at, own, stride=lons)
            for j in range(tiles):
                lines[at * padded : at * padded + own, lane_tile(j)] = (
                    seas[j, rows, :].astype(jnp.float32) * roughs[j, rows, :]
                )
        high, low = halve(lines[...])
        value = dot_half(high, order[...]) + dot_half(low, order[...])
        for at in range(size):
            values[group * size + at] = value[at * padded : (at + 1) * padded]
        start, stop = group * size, (group + 1) * size
        leave(values.at[start:stop], coef.at[start:stop])
        if start < halo:
            until = min(stop, halo)
            leave(values.at[start:until], first.at[start:until])
        if stop > lons - halo:
            since = max(start, lons - halo)
            leave(values.at[since:stop], last.at[since - (lons - halo) : stop - (lons - halo)])
    for copy in leaving:
        copy.wait()


def mixed_at(lons, sums, lon, var):
    value = sums[0][lon // (lons // 2), lon % (lons // 2), var]
    at = plane(lons, lon, var)
    if at is not None:
        for more in sums[1:]:
            value = value + more[at]
    return value


def edge_kernel(lons, halo, parts, passed, *refs):
    sums, coef, (first, last, token) = refs[:parts], refs[parts], refs[parts + 4 + passed : parts + 7 + passed]
    token[...] = jnp.zeros_like(token)
    for lon in range(lons):
        for var in range(2):
            value = coef[lon] * mixed_at(lons, sums, lon, var)
            if lon < halo:
                first[lon, var] = value
            if lon >= lons - halo:
                last[lon - (lons - halo), var] = value


def neighbours(tiles, lane):
    count = len(tiles)
    before = jnp.where(lane == 0, tiles[0], pltpu.roll(tiles[-1], 1, 1))
    after = jnp.where(lane == LANES - 1, tiles[-1], pltpu.roll(tiles[0], LANES - 1, 1))
    line = [before, *tiles, after]
    return [line[j] + line[j + 2] for j in range(count)]


def diffuse(lons, lats, sums, coef, before, after, coef_before, coef_after, rates, weighted, square):
    halo = PASSES
    tiles = lats // LANES
    lane = lax.broadcasted_iota(jnp.int32, (ROWS, LANES), 1)

    for lon in range(lons):
        scale = coef[lon]
        square[halo + lon] = scale * scale
        for var in range(2):
            weighted[0][halo + lon, var] = scale * mixed_at(lons, sums, lon, var)
    for lon in range(halo):
        weighted[0][lon] = before[lon]
        weighted[0][halo + lons + lon] = after[lon]
    for lon in range(halo - 1):
        square[1 + lon] = coef_before[lon] * coef_before[lon]
        square[halo + lons + lon] = coef_after[lon] * coef_after[lon]

    for section in range(PASSES):
        source, target = weighted[section % 2], weighted[(section + 1) % 2]
        rate = rates[section]
        start = section + 1
        stop = lons + 2 * halo - 1 - section

        def one_variable(var, carry):
            def load(lon):
                return [source[lon, var, :, lane_tile(j)] for j in range(tiles)]

            behind, here = load(start - 1), load(start)
            for lon in range(start, stop):
                ahead = load(lon + 1)
                lat = neighbours(here, lane)
                for j in range(tiles):
                    factor = rate * square[lon, :, lane_tile(j)]
                    spread = (behind[j] + ahead[j]) + lat[j] - 4.0 * here[j]
                    target[lon, var, :, lane_tile(j)] = here[j] + factor * spread
                behind, here = here, ahead
            return carry

        lax.fori_loop(0, 2, one_variable, 0)


def diffuse_kernel(lons, lats, parts, *refs):
    sums, rest = refs[:parts], refs[parts:]
    coef, before, after, coef_before, coef_after, rates, back, _, _, out, token, *rest = rest
    *weighted, square, lines = rest
    tiles = lats // LANES
    token[...] = jnp.zeros_like(token)
    diffuse(lons, lats, sums, coef, before, after, coef_before, coef_after, rates, weighted, square)

    count = ROWS * 2 * lons
    for lon in range(lons):
        scale = coef[lon]
        land = scale == 0.0
        inverse = 1.0 / jnp.where(land, 1.0, scale)
        for var in range(2):
            plain = mixed_at(lons, sums, lon, var)
            value = jnp.where(land, plain, weighted[PASSES % 2][PASSES + lon, var] * inverse)
            for j in range(tiles):
                lines[pl.ds(j * count + var * lons + lon, ROWS, stride=2 * lons), :] = value[:, lane_tile(j)]
    high, low = halve(jnp.concatenate([lines[j * count : (j + 1) * count, :] for j in range(tiles)], 1))
    out[...] = jnp.dot(high, back[...], preferred_element_type=jnp.float32) + jnp.dot(
        low, back[...], preferred_element_type=jnp.float32
    )


def whole(*block):
    return pl.BlockSpec(block, lambda i: (0,) * len(block))


def params(mebibytes):
    return pltpu.CompilerParams(vmem_limit_bytes=mebibytes * 1024 * 1024)


def spent(microseconds):
    return pl.CostEstimate(flops=int(microseconds * 1.153e9), bytes_accessed=1024, transcendentals=0)


def on_device(gradient, land_sea, roughness, scale_index, scale_table, balance, corr_a, corr_b):
    own, _, lons, lats = gradient.shape
    levels = balance.shape[0]
    lev_count = lax.axis_size("lev")
    tile_count = lax.axis_size("tile")
    me = lax.axis_index("lev")
    units = -(-own // ROWS)
    padded = units * ROWS
    chunks = chunk_units(units)
    starts = [sum(chunks[:c]) for c in range(len(chunks))]
    offsets = [(s * ROWS, c * ROWS) for s, c in zip(starts, chunks)]
    halo = PASSES
    unit_bytes = lons * 2 * ROWS * lats * 4
    f32 = jnp.float32
    hidden = pl.BlockSpec(memory_space=pl.ANY)

    def along(shift):
        return [(i, (i + shift) % lev_count) for i in range(lev_count)]

    with jax.named_scope("raw"):
        rows = gradient[:, 1, : lons // 2]
        raws = [lax.ppermute(rows, "lev", along(shift)) for shift in range(1, lev_count)]

    tiles = lats // LANES
    place = np.arange(lats)
    order = np.zeros((lats, lats), np.float32)
    order[place, (place % tiles) * LANES + place // tiles] = 1.0
    back = jnp.asarray(order.T, jnp.bfloat16)
    order = jnp.asarray(order, jnp.bfloat16)

    up = [(i, (i + 1) % tile_count) for i in range(tile_count)]
    down = [(j, i) for i, j in up]
    with jax.named_scope("coef"):
        coef, first, last = pl.pallas_call(
            functools.partial(coef_kernel, own, padded, lons, halo - 1, tiles),
            out_shape=[
                jax.ShapeDtypeStruct((lons, padded, lats), f32),
                jax.ShapeDtypeStruct((halo - 1, padded, lats), f32),
                jax.ShapeDtypeStruct((halo - 1, padded, lats), f32),
            ],
            in_specs=[hidden, hidden, pl.BlockSpec(memory_space=pltpu.VMEM), hidden],
            out_specs=[hidden] * 3,
            scratch_shapes=[
                pltpu.VMEM((tiles, own * lons, LANES), jnp.int32),
                pltpu.VMEM((tiles, own * lons, LANES), f32),
                pltpu.VMEM((lons // COEF_GROUPS * padded, lats), f32),
                pltpu.VMEM((lons, padded, lats), f32),
                pltpu.SemaphoreType.DMA((2 * tiles + 3 * COEF_GROUPS,)),
            ],
            compiler_params=params(53),
            cost_estimate=spent(10),
            name="coef",
        )(land_sea.reshape(own * lons, lats), roughness.reshape(own * lons, lats), order, rows)
        coef_before = lax.ppermute(last, "tile", up)
        coef_after = lax.ppermute(first, "tile", down)

    half = lons // 2
    shape = (levels, own, padded, lons, tiles, lev_count)
    kept_shapes = [jax.ShapeDtypeStruct((2, half, 2, size, lats), f32) for _, size in offsets]
    sent_shapes = [jax.ShapeDtypeStruct((3 * half, size, lats), f32) for _, size in offsets]
    kept_specs = [pl.BlockSpec((2, PAIR, 2, size, lats), lambda i: (0, i, 0, 0, 0)) for _, size in offsets]
    sent_specs = [pl.BlockSpec((3 * PAIR, size, lats), lambda i: (i, 0, 0)) for _, size in offsets]
    level_starts = [lax.rem(me + shift, lev_count) * own for shift in range(lev_count)]
    with jax.named_scope("mix"):
        mixed = pl.pallas_call(
            functools.partial(mix_kernel, shape, offsets),
            grid=(half // PAIR,),
            out_shape=kept_shapes + sent_shapes * (lev_count - 1),
            in_specs=[pl.BlockSpec(memory_space=pltpu.SMEM)]
            + [hidden]
            + [whole(levels, levels)] * 3
            + [whole(lats, lats)],
            out_specs=kept_specs + sent_specs * (lev_count - 1),
            scratch_shapes=[
                pltpu.VMEM((2 * lev_count * padded, 6 * padded), jnp.bfloat16),
                pltpu.VMEM(((lev_count + 1) * padded, 6 * padded), jnp.bfloat16),
                pltpu.VMEM((2, PAIR, 2 * padded, lats), f32),
                pltpu.VMEM((2, PAIR * 4 * padded, lats), jnp.bfloat16),
                pltpu.VMEM((2, 6 * padded, PAIR * lats), jnp.bfloat16),
                pltpu.VMEM((tiles, own * 2 * lons, LANES), f32),
                pltpu.SemaphoreType.DMA((tiles,)),
            ],
            compiler_params=params(50),
            cost_estimate=spent(20),
            name="mix",
        )(
            jnp.stack(level_starts),
            gradient.reshape(own * 2 * lons, lats),
            balance,
            corr_a,
            corr_b,
            order,
        )
        sent = [mixed[c + len(chunks) :: len(chunks)] for c in range(len(chunks))]

        def send(arrays):
            return [lax.ppermute(array, "lev", along(shift + 1)) for shift, array in enumerate(arrays)]

        final = len(chunks) - 1
        received = [send(arrays) if c < final or final < 2 else None for c, arrays in enumerate(sent)]

    with jax.named_scope("raw"):
        kept = pl.pallas_call(
            functools.partial(raw_kernel, shape, offsets),
            grid=(half // PAIR,),
            out_shape=kept_shapes,
            in_specs=[pl.BlockSpec(memory_space=pltpu.SMEM)]
            + [pl.BlockSpec((own * half, LANES), lambda i, j=j: (0, j)) for j in range(tiles)] * (lev_count - 1)
            + [whole(levels, levels)] * 3
            + [whole(lats, lats)]
            + [pl.BlockSpec((1, PAIR, 2, size, lats), lambda i: (0, i, 0, 0, 0)) for _, size in offsets],
            out_specs=[pl.BlockSpec((1, PAIR, 2, size, lats), lambda i: (0, i, 0, 0, 0)) for _, size in offsets],
            scratch_shapes=[
                pltpu.VMEM((lev_count - 1, 2 * padded, 3 * padded), jnp.bfloat16),
                pltpu.VMEM((PAIR, padded, lats), f32),
                pltpu.VMEM((PAIR * 2 * padded, lats), jnp.bfloat16),
                pltpu.VMEM((3 * padded, PAIR * lats), jnp.bfloat16),
            ],
            input_output_aliases={5 + tiles * (lev_count - 1) + c: c for c in range(len(chunks))},
            compiler_params=params(16),
            cost_estimate=spent(6),
            name="raw",
        )(
            jnp.stack([level_starts[(lev_count - shift) % lev_count] for shift in range(lev_count)]),
            *[part for raw in raws for part in [raw.reshape(own * half, lats)] * tiles],
            balance,
            corr_a,
            corr_b,
            order,
            *mixed[: len(chunks)],
        )

    with jax.named_scope("rates"):
        own_index = lax.dynamic_slice_in_dim(scale_index, me * own, own, 1)
        picks = own_index[:, :, None] == jnp.arange(NSCALE, dtype=jnp.int32)[None, None, :]
        rates = jnp.sum(picks.astype(f32) * scale_table[None, None, :], -1)
        rates = jnp.pad(rates, ((0, 0), (0, padded - own)))
        rates = jnp.broadcast_to(rates[:, :, None], (PASSES, padded, LANES))

    token_shape = jax.ShapeDtypeStruct((ROWS, LANES), f32)
    token_spec = pl.BlockSpec((ROWS, LANES), lambda i: (0, 0))
    result = jnp.zeros((ROWS, LANES), f32)
    token = result

    def sum_specs(parts):
        own_sum = pl.BlockSpec((2, half, 2, ROWS, lats), lambda i: (0, 0, 0, i, 0))
        return [own_sum] + [pl.BlockSpec((3 * half, ROWS, lats), lambda i: (0, i, 0))] * (parts - 1)

    def edges(c, token, passed):
        sums = [kept[c]] + received[c]
        count, start = chunks[c], starts[c]
        halo_shape = jax.ShapeDtypeStruct((halo, 2, count * ROWS, lats), f32)
        fixed = [jax.ShapeDtypeStruct(array.shape, array.dtype) for array in passed]
        with jax.named_scope("edges"):
            first, last, token, *passed = pl.pallas_call(
                functools.partial(edge_kernel, lons, halo, len(sums), len(passed)),
                grid=(count,),
                out_shape=[halo_shape, halo_shape, token_shape, *fixed],
                in_specs=sum_specs(len(sums))
                + [pl.BlockSpec((lons, ROWS, lats), lambda i: (0, start + i, 0))]
                + [hidden] * (3 + len(passed)),
                out_specs=[pl.BlockSpec((halo, 2, ROWS, lats), lambda i: (0, 0, i, 0))] * 2
                + [token_spec]
                + [hidden] * len(passed),
                input_output_aliases={len(sums) + 4 + i: 3 + i for i in range(len(passed))},
                compiler_params=params(12),
                cost_estimate=spent(2),
                name="edges",
            )(*sums, coef, coef_before, coef_after, token, *passed)
            return lax.ppermute(last, "tile", up), lax.ppermute(first, "tile", down), token, passed

    def diffusion(c, before, after, result, token):
        sums = [kept[c]] + received[c]
        count, start = chunks[c], starts[c]
        fixed = lambda i: (0, 0, i, 0)
        level = lambda i: (0, start + i, 0)
        operands = [*sums, coef, before, after, coef_before, coef_after, rates, back, token, result]
        with jax.named_scope("diffusion"):
            return pl.pallas_call(
                functools.partial(diffuse_kernel, lons, lats, len(sums)),
                grid=(count,),
                out_shape=[jax.ShapeDtypeStruct((own * 2 * lons, lats), f32), token_shape],
                in_specs=sum_specs(len(sums))
                + [pl.BlockSpec((lons, ROWS, lats), level)]
                + [pl.BlockSpec((halo, 2, ROWS, lats), fixed)] * 2
                + [pl.BlockSpec((halo - 1, ROWS, lats), level)] * 2
                + [pl.BlockSpec((PASSES, ROWS, LANES), level), whole(lats, lats), hidden, hidden],
                out_specs=[pl.BlockSpec((ROWS * 2 * lons, lats), lambda i: (start + i, 0)), token_spec],
                scratch_shapes=[
                    pltpu.VMEM((lons + 2 * halo, 2, ROWS, lats), f32),
                    pltpu.VMEM((lons + 2 * halo, 2, ROWS, lats), f32),
                    pltpu.VMEM((lons + 2 * halo, ROWS, lats), f32),
                    pltpu.VMEM((tiles * ROWS * 2 * lons, LANES), f32),
                ],
                input_output_aliases={} if c == 0 else {len(operands) - 1: 0},
                compiler_params=params(18),
                cost_estimate=spent(11),
                name="diffusion",
            )(*operands)

    waiting = None
    for c in range(len(chunks)):
        before, after, token, passed = edges(c, token, sent[final] if c == final - 2 else [])
        if c == final - 2:
            received[final] = send(passed)
        if waiting is not None:
            result, token = diffusion(c - 1, *waiting, result, token)
        waiting = (before, after)
    result, _ = diffusion(len(chunks) - 1, *waiting, result, token)
    return result.reshape(own, 2, lons, lats)


def solution(mesh):
    return jax.shard_map(
        on_device,
        mesh=mesh,
        in_specs=(
            P("lev", None, "tile", None),
            P("lev", "tile", None),
            P("lev", "tile", None),
            P(),
            P(),
            P(),
            P(),
            P(),
        ),
        out_specs=P("lev", None, "tile", None),
        check_vma=False,
    )
```
